512 devices in a mesh: expert: 16 (over y, x), seq: 32 (over z, core).
Axes of the slice: x: 4, y: 4, z: 16, core: 2. Of those that a mesh axis runs over, the one named last changes fastest.
Arguments:
- tokens: bfloat16 [4096, 4096], P('seq', 'expert'), may hold values from -6 to 6
- cotangent: bfloat16 [4096, 4096], P('seq', 'expert'), may hold values from -4 to 4
- route: int32 [4096, 2], P('seq'), may hold values from 0 to 15, all different within a row; in each aligned block of 128 rows (0 to 127, 128 to 255, ...) at most 24 rows name the same one
- route_weight: float32 [4096, 2], P('seq'), may hold values from 0.25 to 1
- mean_gate: bfloat16 [16, 4096, 768], P('expert', 'seq'), may hold values from -0.09375 to 0.09375
- spread_gate: bfloat16 [16, 4096, 768], P('expert', 'seq'), may hold values from 0.0046691895 to 0.015625
- noise_gate: bfloat16 [16, 4096, 768], P('expert', 'seq'), may hold values from -4 to 4
- mean_up: bfloat16 [16, 4096, 768], P('expert', 'seq'), may hold values from -0.09375 to 0.09375
- spread_up: bfloat16 [16, 4096, 768], P('expert', 'seq'), may hold values from 0.0046691895 to 0.015625
- noise_up: bfloat16 [16, 4096, 768], P('expert', 'seq'), may hold values from -4 to 4
- mean_down: bfloat16 [16, 768, 4096], P('expert', None, 'seq'), may hold values from -0.21875 to 0.21875
- spread_down: bfloat16 [16, 768, 4096], P('expert', None, 'seq'), may hold values from 0.010803223 to 0.035888672
- noise_down: bfloat16 [16, 768, 4096], P('expert', None, 'seq'), may hold values from -4 to 4
Outputs:
- mixed_out: bfloat16 [4096, 4096], P('seq', 'expert')
- token_grad: bfloat16 [4096, 4096], P('seq', 'expert')
- grad_mean_gate: float32 [16, 4096, 768], P('expert', 'seq')
- grad_spread_gate: float32 [16, 4096, 768], P('expert', 'seq')
- grad_mean_up: float32 [16, 4096, 768], P('expert', 'seq')
- grad_spread_up: float32 [16, 4096, 768], P('expert', 'seq')
- grad_mean_down: float32 [16, 768, 4096], P('expert', None, 'seq')
- grad_spread_down: float32 [16, 768, 4096], P('expert', None, 'seq')
The draws below stay inside these ranges and needn't reach their ends.
Inputs may be any that keep to these rules, and one draw needn't show every extreme that they name: `route`: the 2 routes of a token name different experts. Within each aligned block of 128 rows (one index of seq), no expert is named by more than 24 routes, a bound that some block reaches.
All inputs are finite; a program needn't handle non-finite values.
Results may differ from the reference program's by a relative error of at most 0.0083.
Values may be sent and summed in bfloat16 or wider, within the bound.
No kernel may reach another device: no remote copies, remote signals or barrier semaphores. Data moves between devices by JAX's collectives and lax.ppermute only.
A program may use at most 64 MiB of HBM per device.

```python
import math
import jax
import jax.numpy as jnp
import numpy as np
from jax import lax

D = 4096
FF = 768
TOP = 2
TOK_GRP = 128
EXPERTS = 16
TOKENS = 4096
CAP = 24
N_SEQ = 32


def shard_levels(own_key, shape, shards, least, high):
    def one(axis_at, shards_of):
        steps = jax.random.uniform(jax.random.fold_in(jax.random.fold_in(own_key, 6), axis_at), (shards_of,), jnp.float32, least / len(shards), high / len(shards))
        return jnp.repeat(jnp.exp(steps), shape[axis_at] // shards_of).reshape((-1,) + (1,) * (len(shape) - axis_at - 1))

    gain = one(*shards[0])
    for cut in shards[1:]:
        gain = gain * one(*cut)
    return gain


def routed_block(key, own, number, rows, number_of, top, most, slope):
    order = jax.random.permutation(key, number_of)
    packed, ordinary = shares(number_of, rows * top, most, slope, True), shares(number_of, rows * top, most, slope, False)
    places = jnp.arange(number_of)

    def named(lengths, rotation):
        used = int((lengths > 0).sum())
        fixed = max(1, used // 4)
        shifted = fixed + (places - fixed + rotation * (used - fixed)) % max(1, number_of - fixed)
        return jnp.zeros((number_of,), jnp.int32).at[order[jnp.where(places < fixed, places, shifted)]].set(jnp.asarray(lengths, jnp.int32))

    lengths = jnp.where(number % 4 == 0, named(packed, number // 4), named(ordinary, number - number // 4 - 1))
    mixed = jax.random.permutation(jax.random.fold_in(own, 3), number_of)
    donor, receiver = mixed[0:number_of // 2 * 2:2], mixed[1:number_of // 2 * 2:2]
    room = jnp.minimum(lengths[donor] - 1, most - lengths[receiver]) // 2
    room = jnp.where((donor == order[0]) | (receiver == order[0]) | (lengths[receiver] == 0), 0, jnp.maximum(room, 0))
    shifted = jax.random.randint(jax.random.fold_in(own, 4), (number_of // 2,), 0, 1 << 20) % (room + 1)
    lengths = lengths.at[donor].add(-shifted).at[receiver].add(shifted)
    members = jnp.searchsorted(jnp.cumsum(lengths), jnp.arange(rows * top), side="right").astype(jnp.int32)
    grid = members.reshape(top, rows).T
    grid = grid[jax.random.permutation(jax.random.fold_in(own, 1), rows)]
    rotation = jax.random.randint(jax.random.fold_in(own, 2), (rows, 1), 0, top)
    return jnp.take_along_axis(grid, (jnp.arange(top)[None, :] + rotation) % top, axis=1)


def shares(count, total, bound, slope, full):
    weights = [(1 << 20) // math.isqrt(grade ** slope) + 1 for grade in range(1, count + 1)]
    largest = bound if full else min(bound, max(-(-total // count), total * weights[0] // sum(weights)))
    least = 1 if total - largest >= count - 1 else 0
    holding, spare = [largest] + [least] * (count - 1), total - largest - least * (count - 1)
    while spare > 0:
        free = [i for i in range(1, count) if holding[i] < largest] or [i for i in range(1, count) if holding[i] < bound]
        mass, budget = sum([weights[i] for i in free]), spare
        for i in free:
            more = min(bound - holding[i], max(1, budget * weights[i] // mass), spare)
            holding[i] = holding[i] + more
            spare = spare - more
    return np.array(holding)


def noise(key, extent, scale, most, pieces=(), kind=jnp.bfloat16):
    result = jax.random.normal(key, extent, jnp.float32) * scale
    if len(pieces) > 0:
        result = shard_levels(key, extent, pieces, -0.22, 0.18) * result
    return jnp.clip(result, min=-most, max=most).astype(kind)


def setup_inputs(seed: int = 0) -> dict:
    streams_of = jax.random.split(jax.random.key(seed), 14)
    tokens = noise(streams_of[0], (TOKENS, D), 1.0, 6.0, ((0, 32), (1, 16)))
    cotangent = noise(streams_of[1], (TOKENS, D), 0.5, 4.0, ((0, 32), (1, 16)))
    route_keys = jax.random.split(jax.random.fold_in(streams_of[2], 1), TOKENS // TOK_GRP)
    route_turns = jax.random.permutation(jax.random.fold_in(streams_of[2], 3), TOKENS // TOK_GRP)
    route = jax.vmap(lambda own, number: routed_block(jax.random.fold_in(streams_of[2], 2), own, number, TOK_GRP, EXPERTS, TOP, CAP, 2))(route_keys, route_turns).reshape((TOKENS, TOP))
    route_weight = jnp.clip(0.25 + 0.75 * jax.random.uniform(streams_of[3], (TOKENS, TOP), jnp.float32) ** shard_levels(streams_of[3], (TOKENS, TOP), ((0, 32),), -0.2, 0.2), 0.25, 1.0)
    mean_gate = noise(streams_of[4], (EXPERTS, D, FF), D ** -0.5, 0.09375, ((0, 16), (1, 32)))
    spread_gate = jnp.clip(jnp.exp(math.log(0.015625) - 1.2078867 * jax.random.uniform(streams_of[5], (EXPERTS, D, FF), jnp.float32) ** shard_levels(streams_of[5], (EXPERTS, D, FF), ((0, 16), (1, 32)), -0.2, 0.2)), 0.0046691895, 0.015625).astype(jnp.bfloat16)
    noise_gate = noise(streams_of[6], (EXPERTS, D, FF), 1.0, 4.0, ((0, 16), (1, 32)))
    mean_up = noise(streams_of[7], (EXPERTS, D, FF), D ** -0.5, 0.09375, ((0, 16), (1, 32)))
    spread_up = jnp.clip(jnp.exp(math.log(0.015625) - 1.2078867 * jax.random.uniform(streams_of[8], (EXPERTS, D, FF), jnp.float32) ** shard_levels(streams_of[8], (EXPERTS, D, FF), ((0, 16), (1, 32)), -0.2, 0.2)), 0.0046691895, 0.015625).astype(jnp.bfloat16)
    noise_up = noise(streams_of[9], (EXPERTS, D, FF), 1.0, 4.0, ((0, 16), (1, 32)))
    mean_down = noise(streams_of[10], (EXPERTS, FF, D), FF ** -0.5, 0.21875, ((0, 16), (2, 32)))
    spread_down = jnp.clip(jnp.exp(math.log(0.035888672) - 1.2005772 * jax.random.uniform(streams_of[11], (EXPERTS, FF, D), jnp.float32) ** shard_levels(streams_of[11], (EXPERTS, FF, D), ((0, 16), (2, 32)), -0.2, 0.2)), 0.010803223, 0.035888672).astype(jnp.bfloat16)
    noise_down = noise(streams_of[12], (EXPERTS, FF, D), 1.0, 4.0, ((0, 16), (2, 32)))
    return dict(tokens=tokens, cotangent=cotangent, route=route, route_weight=route_weight, mean_gate=mean_gate, spread_gate=spread_gate, noise_gate=noise_gate, mean_up=mean_up, spread_up=spread_up, noise_up=noise_up, mean_down=mean_down, spread_down=spread_down, noise_down=noise_down)


def slot_targets(route):
    per_group = route.reshape(N_SEQ, TOK_GRP * TOP)
    choose = (per_group[:, :, None] == jnp.arange(EXPERTS, dtype=jnp.int32)[None, None, :]).astype(jnp.int32)
    earlier = jnp.cumsum(choose, axis=1) - choose
    position = jnp.sum(earlier * choose, axis=2).astype(jnp.int32)
    group_ids = jnp.arange(N_SEQ, dtype=jnp.int32)[:, None]
    target = per_group * (CAP * N_SEQ) + group_ids * CAP + position
    return target.reshape(-1).astype(jnp.int32)


def sampled(mean_part, spread, noise_part):
    return (mean_part.astype(jnp.float32) + spread.astype(jnp.float32) * noise_part.astype(jnp.float32)).astype(jnp.bfloat16)


def expert_pass(operands):
    slot_x, slot_d, mean_g, spread_g, noise_g, mean_u, spread_u, noise_u, mean_d, spread_d, noise_d = operands
    w_gate = sampled(mean_g, spread_g, noise_g)
    w_up = sampled(mean_u, spread_u, noise_u)
    w_down = sampled(mean_d, spread_d, noise_d)
    w_both = jnp.concatenate([w_gate, w_up], axis=1)
    summed = jnp.dot(slot_x, w_both, preferred_element_type=jnp.float32)
    back_hidden = lax.dot_general(slot_d, w_down, (((1,), (1,)), ((), ())), preferred_element_type=jnp.float32)
    gate_val = summed[:, :FF]
    up_val = summed[:, FF:]
    sigmoid_gate = jax.nn.sigmoid(gate_val)
    active = gate_val * sigmoid_gate
    hidden = (active * up_val).astype(jnp.bfloat16)
    grad_gate = (back_hidden * up_val * sigmoid_gate * (1.0 + gate_val * (1.0 - sigmoid_gate))).astype(jnp.bfloat16)
    grad_upper = (back_hidden * active).astype(jnp.bfloat16)
    slot_out = jnp.dot(hidden, w_down, preferred_element_type=jnp.float32).astype(jnp.bfloat16)
    down_grad = lax.dot_general(hidden, slot_d, (((0,), (0,)), ((), ())), preferred_element_type=jnp.float32)
    both_grad = jnp.concatenate([grad_gate, grad_upper], axis=1)
    pair_grad = lax.dot_general(slot_x, both_grad, (((0,), (0,)), ((), ())), preferred_element_type=jnp.float32)
    slot_back = lax.dot_general(both_grad, w_both, (((1,), (1,)), ((), ())), preferred_element_type=jnp.float32).astype(jnp.bfloat16)
    gate_grad = pair_grad[:, :FF]
    up_grad = pair_grad[:, FF:]
    return (slot_out, slot_back, gate_grad, gate_grad * noise_g.astype(jnp.float32),
            up_grad, up_grad * noise_u.astype(jnp.float32),
            down_grad, down_grad * noise_d.astype(jnp.float32))


def reference(tokens, cotangent, route, route_weight, mean_gate, spread_gate, noise_gate, mean_up, spread_up, noise_up, mean_down, spread_down, noise_down):
    target = slot_targets(route)
    token_ids = (jnp.arange(TOKENS * TOP, dtype=jnp.int32) // TOP).astype(jnp.int32)
    slot_total = EXPERTS * CAP * N_SEQ
    weights = route_weight.reshape(-1)
    slot_x = jnp.zeros((slot_total, D), jnp.bfloat16).at[target].set(tokens[token_ids])
    scaled = (weights[:, None] * cotangent[token_ids].astype(jnp.float32)).astype(jnp.bfloat16)
    slot_d = jnp.zeros((slot_total, D), jnp.bfloat16).at[target].set(scaled)
    slot_shape = (EXPERTS, CAP * N_SEQ, D)
    results = lax.map(expert_pass, (slot_x.reshape(slot_shape), slot_d.reshape(slot_shape),
                                    mean_gate, spread_gate, noise_gate, mean_up, spread_up, noise_up,
                                    mean_down, spread_down, noise_down))
    slot_out = results[0].reshape(slot_total, D)
    slot_back = results[1].reshape(slot_total, D)
    mixed_out = jnp.sum((weights[:, None] * slot_out[target].astype(jnp.float32)).reshape(TOKENS, TOP, D), axis=1).astype(jnp.bfloat16)
    token_grad = jnp.sum(slot_back[target].astype(jnp.float32).reshape(TOKENS, TOP, D), axis=1).astype(jnp.bfloat16)
    return (mixed_out, token_grad, results[2], results[3], results[4], results[5], results[6], results[7])
```

```python
import jax
import jax.numpy as jnp
from jax import lax
from jax.sharding import Mesh, PartitionSpec as P

BF = jnp.bfloat16
F32 = jnp.float32
PLANE = ("y", "x")
RING = ("za", "zb", "core")
QUAD = 4


def sampled(mean_part, spread, noise_part):
    return (mean_part.astype(F32) + spread.astype(F32) * noise_part.astype(F32)).astype(BF)


def contract(left_side, right_side, left_dim, right_dim):
    return lax.dot_general(
        left_side,
        right_side,
        (((left_dim,), (right_dim,)), ((), ())),
        preferred_element_type=F32,
    )


def shift(value, step):
    return lax.ppermute(value, "za", [(i, (i + step) % QUAD) for i in range(QUAD)])


def place_routes(route, experts, capacity):
    rows = route.shape[0]
    names = lax.broadcasted_iota(jnp.int32, (rows, experts), 1)
    first = (route[:, 0:1] == names).astype(BF)
    second = (route[:, 1:2] == names).astype(BF)
    below = (
        lax.broadcasted_iota(jnp.int32, (rows, rows), 0)
        > lax.broadcasted_iota(jnp.int32, (rows, rows), 1)
    ).astype(BF)
    earlier = contract(below, first + second, 1, 0)
    place_first = jnp.sum(earlier * first.astype(F32), axis=1, keepdims=True)
    place_second = jnp.sum(
        (earlier + first.astype(F32)) * second.astype(F32), axis=1, keepdims=True
    )
    slots = lax.broadcasted_iota(jnp.int32, (rows, experts * capacity), 1)
    one = (route[:, 0:1] * capacity + place_first.astype(jnp.int32) == slots).astype(BF)
    two = (route[:, 1:2] * capacity + place_second.astype(jnp.int32) == slots).astype(BF)
    return one, two


def activate(total, width):
    gate_val = total[:, :width]
    up_val = total[:, width : 2 * width]
    back_hidden = total[:, 2 * width :]
    sigmoid_gate = jax.nn.sigmoid(gate_val)
    active = gate_val * sigmoid_gate
    hidden = (active * up_val).astype(BF)
    grad_gate = (
        back_hidden * up_val * sigmoid_gate * (1.0 + gate_val * (1.0 - sigmoid_gate))
    ).astype(BF)
    grad_upper = (back_hidden * active).astype(BF)
    return jnp.concatenate([grad_gate, grad_upper, hidden], axis=1)


def body(
    tokens,
    cotangent,
    route,
    route_weight,
    mean_gate,
    spread_gate,
    noise_gate,
    mean_up,
    spread_up,
    noise_up,
    mean_down,
    spread_down,
    noise_down,
):
    experts = lax.axis_size(PLANE)
    quads = lax.axis_size("zb")
    group_rows, routes = route.shape
    feats = tokens.shape[1]
    half = feats // 2
    width = mean_gate.shape[2]
    cap = group_rows * routes // experts * 3 // 2
    me = lax.axis_index("za")
    core = lax.axis_index("core")

    w_local = jnp.concatenate(
        [
            sampled(mean_gate[0], spread_gate[0], noise_gate[0]),
            sampled(mean_up[0], spread_up[0], noise_up[0]),
            sampled(mean_down[0], spread_down[0], noise_down[0]).T,
        ],
        axis=1,
    )
    weights = lax.all_gather(w_local, "zb", axis=0, tiled=True)
    w_both = weights[:, : 2 * width]
    w_down = weights[:, 2 * width :]

    one, two = place_routes(route, experts, cap)
    cot = cotangent.astype(F32)
    scaled = jnp.concatenate(
        [
            (route_weight[:, 0:1] * cot).astype(BF),
            (route_weight[:, 1:2] * cot).astype(BF),
        ],
        axis=0,
    )
    send_x = contract(one + two, tokens, 0, 0).astype(BF)
    send_d = contract(jnp.concatenate([one, two], axis=0), scaled, 0, 0).astype(BF)
    send = jnp.concatenate([send_x, send_d], axis=1).reshape(experts, cap, 2 * feats)
    got = lax.all_to_all(send, PLANE, split_axis=0, concat_axis=0, tiled=True)
    got = got.reshape(QUAD, quads, cap, 2, 2, half).transpose(4, 0, 2, 3, 1, 5)
    got = got.reshape(2 * QUAD, cap, 2 * quads * half)
    got = lax.all_to_all(got, ("core", "za"), split_axis=0, concat_axis=0, tiled=True)
    slots = got.reshape(2 * QUAD * cap, 2 * quads * half)
    slot_x = slots[:, : quads * half]
    slot_d = slots[:, quads * half :]

    part = jnp.concatenate(
        [contract(slot_x, w_both, 1, 0), contract(slot_d, w_down, 1, 0)], axis=1
    ).reshape(2, QUAD, cap, 3 * width)
    mine = lax.dynamic_index_in_dim(part, core, 0, keepdims=False)
    other = lax.dynamic_index_in_dim(part, 1 - core, 0, keepdims=False).astype(BF)
    part = mine + lax.ppermute(other, "core", [(0, 1), (1, 0)]).astype(F32)

    def piece(step):
        return lax.dynamic_index_in_dim(part, (me + step) % QUAD, 0, keepdims=False)

    cut = 3 * width // 2
    far = piece(2).astype(BF)
    from_left = shift(far[:, :cut], 1).astype(F32)
    from_right = shift(far[:, cut:], -1).astype(F32)
    ahead = piece(1)
    ahead = jnp.concatenate([ahead[:, :cut] + from_left, ahead[:, cut:]], axis=1).astype(BF)
    behind = piece(3)
    behind = jnp.concatenate([behind[:, :cut], behind[:, cut:] + from_right], axis=1).astype(BF)
    total = piece(0) + shift(ahead, 1).astype(F32) + shift(behind, -1).astype(F32)

    rows = lax.all_gather(activate(total, width), "za", axis=0, tiled=True)
    rows = lax.all_gather(rows, "core", axis=0, tiled=True)
    grads = rows[:, : 2 * width]
    hidden = rows[:, 2 * width :]

    w_grads = jnp.concatenate(
        [contract(slot_x, grads, 0, 0).astype(BF), contract(slot_d, hidden, 0, 0).astype(BF)],
        axis=1,
    )
    w_grads = lax.psum_scatter(w_grads, "zb", scatter_dimension=0, tiled=True)

    outs = jnp.concatenate(
        [contract(hidden, w_down, 1, 1).astype(BF), contract(grads, w_both, 1, 1).astype(BF)],
        axis=1,
    ).reshape(2 * QUAD, cap, 2 * quads * half)
    home = lax.all_to_all(outs, ("core", "za"), split_axis=0, concat_axis=0, tiled=True)
    home = home.reshape(2, QUAD, cap, 2, quads, half).transpose(1, 4, 2, 3, 0, 5)
    home = home.reshape(experts, cap, 2 * feats)
    home = lax.all_to_all(home, PLANE, split_axis=0, concat_axis=0, tiled=True)
    home = home.reshape(experts * cap, 2 * feats)
    out_one = contract(one, home[:, :feats], 1, 0)
    out_two = contract(two, home[:, :feats], 1, 0)
    mixed_out = (route_weight[:, 0:1] * out_one + route_weight[:, 1:2] * out_two).astype(BF)
    token_grad = contract(one + two, home[:, feats:], 1, 0).astype(BF)

    w_grads = w_grads.astype(F32)
    gate_grad = w_grads[:, :width]
    up_grad = w_grads[:, width : 2 * width]
    down_grad = w_grads[:, 2 * width :].T
    return (
        mixed_out,
        token_grad,
        gate_grad[None],
        (gate_grad * noise_gate[0].astype(F32))[None],
        up_grad[None],
        (up_grad * noise_up[0].astype(F32))[None],
        down_grad[None],
        (down_grad * noise_down[0].astype(F32))[None],
    )


def solution(mesh):
    fine = Mesh(mesh.devices.reshape(4, 4, QUAD, 4, 2), PLANE + RING)
    by_token = P(RING, PLANE)
    by_group = P(RING, None)
    by_row = P(PLANE, RING, None)
    by_column = P(PLANE, None, RING)
    return jax.shard_map(
        body,
        mesh=fine,
        in_specs=(by_token,) * 2 + (by_group,) * 2 + (by_row,) * 6 + (by_column,) * 3,
        out_specs=(by_token,) * 2 + (by_row,) * 4 + (by_column,) * 2,
        check_vma=False,
    )
```

```python
import jax
import jax.numpy as jnp
from jax import lax
from jax.experimental import pallas as pl
from jax.experimental.pallas import tpu as pltpu
from jax.sharding import Mesh, PartitionSpec as P

BF = jnp.bfloat16
F32 = jnp.float32
PLANE = ("y", "x")
RING = ("za", "zb", "core")
QUAD = 4
WINDOW = ((0, 1, -1, 2), (0, 1, -1, -2))


def sampled(mean_part, spread, noise_part):
    return (mean_part.astype(F32) + spread.astype(F32) * noise_part.astype(F32)).astype(BF)


def contract(left_side, right_side, left_dim, right_dim):
    return lax.dot_general(
        left_side,
        right_side,
        (((left_dim,), (right_dim,)), ((), ())),
        preferred_element_type=F32,
    )


def shift(value, step):
    return lax.ppermute(value, "za", [(i, (i + step) % QUAD) for i in range(QUAD)])


def along_ring(value, steps):
    chips = lax.axis_size("za") * lax.axis_size("zb")
    pairs = [
        (2 * z + core, 2 * ((z + steps[core]) % chips) + core)
        for z in range(chips)
        for core in range(2)
    ]
    return lax.ppermute(value, RING, pairs)


def kernel_call(kernel, outs, *operands, free=0, scalars=0):
    whole = pl.BlockSpec(memory_space=pltpu.VMEM)
    count = len(operands) - free - scalars
    moved = sum(a.size * a.dtype.itemsize for a in operands) + sum(
        o.size * o.dtype.itemsize for o in outs
    )
    return pl.pallas_call(
        kernel,
        out_shape=tuple(outs),
        in_specs=[pl.BlockSpec(memory_space=pltpu.SMEM)] * scalars
        + [whole] * count
        + [pl.BlockSpec(memory_space=pl.ANY)] * free,
        out_specs=(whole,) * len(outs),
        compiler_params=pltpu.CompilerParams(vmem_limit_bytes=8 * 1024 * 1024),
        cost_estimate=pl.CostEstimate(flops=0, bytes_accessed=moved, transcendentals=0),
    )(*operands)


def sample_kernel(mg, sg, ng, mu, su, nu, md, sd, nd, out):
    width = mg.shape[2]
    out[:, :width] = sampled(mg[0], sg[0], ng[0])
    out[:, width : 2 * width] = sampled(mu[0], su[0], nu[0])
    down = md[0].astype(F32) + sd[0].astype(F32) * nd[0].astype(F32)
    out[:, 2 * width :] = down.T.astype(BF)


def spread_kernel(where, got, *rest):
    out = rest[-1]
    chips, half = got.shape[0], got.shape[2] // 4
    for core in range(2):
        for za in range(QUAD):
            for at, step in enumerate(WINDOW[core]):
                chip = lax.rem(where[0] + (4 * za + step + chips), chips)
                for kind in range(2):
                    lane = (4 * kind + at) * half
                    here = (2 * kind + core) * half
                    out[core * QUAD + za, :, lane : lane + half] = got[
                        chip, :, here : here + half
                    ]


def collect_kernel(where, got, out):
    chips, half = out.shape[0], out.shape[2] // 4
    for core in range(2):
        for za in range(QUAD):
            for at, step in enumerate(WINDOW[core]):
                chip = lax.rem(where[0] + (4 * za + step + chips), chips)
                for kind in range(2):
                    lane = (4 * kind + at) * half
                    here = (2 * kind + core) * half
                    out[chip, :, here : here + half] = got[
                        core * QUAD + za, :, lane : lane + half
                    ]


def forward_kernel(where, slots, w0, w1, w2, w3, mine, other):
    quads, cap, width = mine.shape[0], mine.shape[1], w0.shape[1] // 3
    rows, half = quads * cap, w0.shape[0]
    core = where[0]
    for side, out in ((core, mine), (1 - core, other)):
        start = pl.multiple_of(side * rows, rows)
        for part in range(3):
            kind = part // 2
            total = None
            for at, w in enumerate((w0, w1, w2, w3)):
                lane = (4 * kind + at) * half
                term = contract(
                    slots[pl.ds(start, rows), lane : lane + half],
                    w[:, part * width : (part + 1) * width],
                    1,
                    0,
                )
                total = term if total is None else total + term
            for quad in range(quads):
                out[quad, :, part * width : (part + 1) * width] = total[
                    quad * cap : (quad + 1) * cap
                ].astype(out.dtype)


def split_kernel(where, mine, other, far_right, far_left, own, ahead, behind):
    me, cut = where[0], far_right.shape[1]

    def piece(step, lanes):
        at = jnp.bitwise_and(me + step, QUAD - 1)
        return mine[at, :, lanes] + other[at, :, lanes].astype(F32)

    whole = slice(0, 2 * cut)
    far_right[...] = piece(2, slice(0, cut)).astype(BF)
    far_left[...] = piece(2, slice(cut, 2 * cut)).astype(BF)
    own[...] = piece(0, whole)
    ahead[...] = piece(1, whole)
    behind[...] = piece(3, whole)


def relay_kernel(ahead, behind, from_left, from_right, to_right, to_left):
    cut = from_left.shape[1]
    to_right[:, :cut] = (ahead[:, :cut] + from_left[...].astype(F32)).astype(BF)
    to_right[:, cut:] = ahead[:, cut:].astype(BF)
    to_left[:, :cut] = behind[:, :cut].astype(BF)
    to_left[:, cut:] = (behind[:, cut:] + from_right[...].astype(F32)).astype(BF)


def activate_kernel(own, from_left, from_right, out):
    width = own.shape[1] // 3

    def total(start):
        lanes = slice(start, start + width)
        return own[:, lanes] + from_left[:, lanes].astype(F32) + from_right[:, lanes].astype(F32)

    gate_val, up_val, back_hidden = total(0), total(width), total(2 * width)
    sigmoid_gate = jax.nn.sigmoid(gate_val)
    active = gate_val * sigmoid_gate
    out[:, :width] = (
        back_hidden * up_val * sigmoid_gate * (1.0 + gate_val * (1.0 - sigmoid_gate))
    ).astype(BF)
    out[:, width : 2 * width] = (back_hidden * active).astype(BF)
    out[:, 2 * width :] = (active * up_val).astype(BF)


def outs_kernel(rows, w0, w1, w2, w3, out):
    width, half = w0.shape[1] // 3, w0.shape[0]
    for at, w in enumerate((w0, w1, w2, w3)):
        value = contract(rows[:, 2 * width :], w[:, 2 * width :], 1, 1)
        out[:, at * half : (at + 1) * half] = value.astype(BF)
        value = contract(rows[:, : 2 * width], w[:, : 2 * width], 1, 1)
        out[:, (4 + at) * half : (5 + at) * half] = value.astype(BF)


def grads_kernel(slots, rows, after, g0, g1, g2, g3):
    del after
    width, half = g0.shape[1] // 3, g0.shape[0]
    for at, g in enumerate((g0, g1, g2, g3)):
        left = slots[:, at * half : (at + 1) * half]
        value = contract(left, rows[:, : 2 * width], 0, 0)
        g[:, : 2 * width] = value.astype(g.dtype)
        left = slots[:, (4 + at) * half : (5 + at) * half]
        value = contract(left, rows[:, 2 * width :], 0, 0)
        g[:, 2 * width :] = value.astype(g.dtype)


def finish_kernel(g0, g1, g2, g3, ng, nu, nd, mg, sg, mu, su, md, sd):
    width = ng.shape[2]

    def total(start):
        lanes = slice(start, start + width)
        return (g0[:, lanes] + g1[:, lanes].astype(F32)) + (
            g2[:, lanes].astype(F32) + g3[:, lanes].astype(F32)
        )

    gate = total(0)
    mg[0] = gate
    sg[0] = gate * ng[0].astype(F32)
    up = total(width)
    mu[0] = up
    su[0] = up * nu[0].astype(F32)
    down = total(2 * width).T
    md[0] = down
    sd[0] = down * nd[0].astype(F32)


def place_routes(route, experts, capacity):
    rows = route.shape[0]
    names = lax.broadcasted_iota(jnp.int32, (rows, experts), 1)
    first = (route[:, 0:1] == names).astype(BF)
    second = (route[:, 1:2] == names).astype(BF)
    below = (
        lax.broadcasted_iota(jnp.int32, (rows, rows), 0)
        > lax.broadcasted_iota(jnp.int32, (rows, rows), 1)
    ).astype(BF)
    earlier = contract(below, first + second, 1, 0)
    place_first = jnp.sum(earlier * first.astype(F32), axis=1, keepdims=True)
    place_second = jnp.sum(
        (earlier + first.astype(F32)) * second.astype(F32), axis=1, keepdims=True
    )
    slots = lax.broadcasted_iota(jnp.int32, (rows, experts * capacity), 1)
    one = (route[:, 0:1] * capacity + place_first.astype(jnp.int32) == slots).astype(BF)
    two = (route[:, 1:2] * capacity + place_second.astype(jnp.int32) == slots).astype(BF)
    return one, two


def body(
    tokens,
    cotangent,
    route,
    route_weight,
    mean_gate,
    spread_gate,
    noise_gate,
    mean_up,
    spread_up,
    noise_up,
    mean_down,
    spread_down,
    noise_down,
):
    experts = lax.axis_size(PLANE)
    group_rows, routes = route.shape
    feats = tokens.shape[1]
    half = feats // 2
    width = mean_gate.shape[2]
    cap = group_rows * routes // experts * 3 // 2
    rows_all = 2 * QUAD * cap
    me = lax.axis_index("za").astype(jnp.int32).reshape(1)
    zb = lax.axis_index("zb").astype(jnp.int32).reshape(1)
    core = lax.axis_index("core").astype(jnp.int32).reshape(1)

    (w_own,) = kernel_call(
        sample_kernel,
        [jax.ShapeDtypeStruct((half, 3 * width), BF)],
        mean_gate,
        spread_gate,
        noise_gate,
        mean_up,
        spread_up,
        noise_up,
        mean_down,
        spread_down,
        noise_down,
    )
    weights = (
        w_own,
        along_ring(w_own, (-1, -1)),
        along_ring(w_own, (1, 1)),
        along_ring(w_own, (-2, 2)),
    )

    one, two = place_routes(route, experts, cap)
    cot = cotangent.astype(F32)
    scaled = jnp.concatenate(
        [
            (route_weight[:, 0:1] * cot).astype(BF),
            (route_weight[:, 1:2] * cot).astype(BF),
        ],
        axis=0,
    )
    send_x = contract(one + two, tokens, 0, 0).astype(BF)
    send_d = contract(jnp.concatenate([one, two], axis=0), scaled, 0, 0).astype(BF)
    send = jnp.concatenate([send_x, send_d], axis=1).reshape(experts, cap, 2 * feats)
    got = lax.all_to_all(send, PLANE, split_axis=0, concat_axis=0, tiled=True)
    (got,) = kernel_call(
        spread_kernel,
        [jax.ShapeDtypeStruct((2 * QUAD, cap, 8 * half), BF)],
        zb,
        got,
        *weights[1:],
        scalars=1,
        free=3,
    )
    got = lax.all_to_all(got, ("core", "za"), split_axis=0, concat_axis=0, tiled=True)
    slots = got.reshape(rows_all, 8 * half)

    mine, other = kernel_call(
        forward_kernel,
        [
            jax.ShapeDtypeStruct((QUAD, cap, 3 * width), F32),
            jax.ShapeDtypeStruct((QUAD, cap, 3 * width), BF),
        ],
        core,
        slots,
        *weights,
        scalars=1,
    )
    other = lax.ppermute(other, "core", [(0, 1), (1, 0)])
    cut = 3 * width // 2
    total = jax.ShapeDtypeStruct((cap, 3 * width), F32)
    wire = jax.ShapeDtypeStruct((cap, 3 * width), BF)
    half_wire = jax.ShapeDtypeStruct((cap, cut), BF)
    far_right, far_left, own, ahead, behind = kernel_call(
        split_kernel, [half_wire] * 2 + [total] * 3, me, mine, other, scalars=1
    )
    to_right, to_left = kernel_call(
        relay_kernel, [wire] * 2, ahead, behind, shift(far_right, 1), shift(far_left, -1)
    )
    (rows,) = kernel_call(
        activate_kernel, [wire], own, shift(to_right, 1), shift(to_left, -1)
    )

    rows = lax.all_gather(rows, "za", axis=0, tiled=True)
    rows = lax.all_gather(rows, "core", axis=0, tiled=True)
    (outs,) = kernel_call(
        outs_kernel, [jax.ShapeDtypeStruct((rows_all, 8 * half), BF)], rows, *weights
    )
    outs = outs.reshape(2 * QUAD, cap, 8 * half)
    home = lax.all_to_all(outs, ("core", "za"), split_axis=0, concat_axis=0, tiled=True)

    w_grads = kernel_call(
        grads_kernel,
        [jax.ShapeDtypeStruct((half, 3 * width), F32)]
        + [jax.ShapeDtypeStruct((half, 3 * width), BF)] * 3,
        slots,
        rows,
        home,
        free=1,
    )
    w_grads = (
        w_grads[0],
        along_ring(w_grads[1], (1, 1)),
        along_ring(w_grads[2], (-1, -1)),
        along_ring(w_grads[3], (2, -2)),
    )

    (home,) = kernel_call(
        collect_kernel,
        [jax.ShapeDtypeStruct((experts, cap, 2 * feats), BF)],
        zb,
        home,
        scalars=1,
    )
    home = lax.all_to_all(home, PLANE, split_axis=0, concat_axis=0, tiled=True)
    home = home.reshape(experts * cap, 2 * feats)
    out_one = contract(one, home[:, :feats], 1, 0)
    out_two = contract(two, home[:, :feats], 1, 0)
    mixed_out = (route_weight[:, 0:1] * out_one + route_weight[:, 1:2] * out_two).astype(BF)
    token_grad = contract(one + two, home[:, feats:], 1, 0).astype(BF)

    by_row = jax.ShapeDtypeStruct((1, half, width), F32)
    by_column = jax.ShapeDtypeStruct((1, width, half), F32)
    ends = kernel_call(
        finish_kernel,
        [by_row] * 4 + [by_column] * 2,
        *w_grads,
        noise_gate,
        noise_up,
        noise_down,
    )
    return (mixed_out, token_grad) + tuple(ends)


def solution(mesh):
    fine = Mesh(mesh.devices.reshape(4, 4, QUAD, 4, 2), PLANE + RING)
    by_token = P(RING, PLANE)
    by_group = P(RING, None)
    by_row = P(PLANE, RING, None)
    by_column = P(PLANE, None, RING)
    return jax.shard_map(
        body,
        mesh=fine,
        in_specs=(by_token,) * 2 + (by_group,) * 2 + (by_row,) * 6 + (by_column,) * 3,
        out_specs=(by_token,) * 2 + (by_row,) * 4 + (by_column,) * 2,
        check_vma=False,
    )
```

```python
import jax
import jax.numpy as jnp
from jax import lax
from jax.experimental import pallas as pl
from jax.experimental.pallas import tpu as pltpu
from jax.sharding import Mesh, PartitionSpec as P

BF = jnp.bfloat16
F32 = jnp.float32
PLANE = ("y", "x")
RING = ("za", "zb", "core")
QUAD = 4
WINDOW = ((0, 1, -1, 2), (0, 1, -1, -2))


def sampled(mean_part, spread, noise_part):
    return (mean_part.astype(F32) + spread.astype(F32) * noise_part.astype(F32)).astype(BF)


def contract(left_side, right_side, left_dim, right_dim):
    return lax.dot_general(
        left_side,
        right_side,
        (((left_dim,), (right_dim,)), ((), ())),
        preferred_element_type=F32,
    )


def shift(value, step):
    return lax.ppermute(value, "za", [(i, (i + step) % QUAD) for i in range(QUAD)])


def along_ring(value, steps):
    chips = lax.axis_size("za") * lax.axis_size("zb")
    pairs = [
        (2 * z + core, 2 * ((z + steps[core]) % chips) + core)
        for z in range(chips)
        for core in range(2)
    ]
    return lax.ppermute(value, RING, pairs)


def kernel_call(kernel, outs, *operands, free=0, scalars=0, scratch=()):
    whole = pl.BlockSpec(memory_space=pltpu.VMEM)
    count = len(operands) - free - scalars
    moved = sum(a.size * a.dtype.itemsize for a in operands) + sum(
        o.size * o.dtype.itemsize for o in outs
    )
    return pl.pallas_call(
        kernel,
        out_shape=tuple(outs),
        in_specs=[pl.BlockSpec(memory_space=pltpu.SMEM)] * scalars
        + [whole] * count
        + [pl.BlockSpec(memory_space=pl.ANY)] * free,
        out_specs=(whole,) * len(outs),
        scratch_shapes=list(scratch),
        compiler_params=pltpu.CompilerParams(vmem_limit_bytes=8 * 1024 * 1024),
        cost_estimate=pl.CostEstimate(flops=0, bytes_accessed=moved, transcendentals=0),
    )(*operands)


def sample_kernel(*refs):
    sources, out, rows, columns, done = refs[:9], refs[9], refs[10], refs[11], refs[12]
    places = [rows.at[i] for i in range(6)] + [columns.at[i] for i in range(3)]
    copies = [
        pltpu.make_async_copy(source.at[0], place, done.at[i])
        for i, (source, place) in enumerate(zip(sources, places))
    ]
    for copy in copies:
        copy.start()
    width = rows.shape[2]
    for part in range(2):
        for copy in copies[3 * part : 3 * part + 3]:
            copy.wait()
        out[:, part * width : (part + 1) * width] = sampled(
            rows[3 * part], rows[3 * part + 1], rows[3 * part + 2]
        )
    for copy in copies[6:]:
        copy.wait()
    down = columns[0].astype(F32) + columns[1].astype(F32) * columns[2].astype(F32)
    out[:, 2 * width :] = down.T.astype(BF)


def pick_kernel(route, weight, tokens, cotangent, out):
    experts, cap, feats = out.shape[0], out.shape[1], tokens.shape[1]
    one, two = place_routes(route[...], experts, cap)
    cot = cotangent[...].astype(F32)
    x = contract(one + two, tokens[...], 0, 0).astype(BF)
    d = (
        contract(one, (weight[:, 0:1] * cot).astype(BF), 0, 0)
        + contract(two, (weight[:, 1:2] * cot).astype(BF), 0, 0)
    ).astype(BF)
    for expert in range(experts):
        rows = slice(expert * cap, (expert + 1) * cap)
        out[expert, :, :feats] = x[rows]
        out[expert, :, feats:] = d[rows]


def spread_kernel(where, got, *rest):
    out = rest[-1]
    chips, half = got.shape[0], got.shape[2] // 4
    for core in range(2):
        for za in range(QUAD):
            for at, step in enumerate(WINDOW[core]):
                chip = lax.rem(where[0] + (4 * za + step + chips), chips)
                for kind in range(2):
                    lane = (4 * kind + at) * half
                    here = (2 * kind + core) * half
                    out[core * QUAD + za, :, lane : lane + half] = got[
                        chip, :, here : here + half
                    ]


def collect_kernel(where, got, *rest):
    out = rest[-1]
    chips, half = out.shape[0], out.shape[2] // 4
    for core in range(2):
        for za in range(QUAD):
            for at, step in enumerate(WINDOW[core]):
                chip = lax.rem(where[0] + (4 * za + step + chips), chips)
                for kind in range(2):
                    lane = (4 * kind + at) * half
                    here = (2 * kind + core) * half
                    out[chip, :, here : here + half] = got[
                        core * QUAD + za, :, lane : lane + half
                    ]


def partial_sum(slots, weights, side, rows, part):
    width, half = weights[0].shape[1] // 3, weights[0].shape[0]
    start = pl.multiple_of(side * rows, rows)
    total = None
    for at, w in enumerate(weights):
        lane = (4 * (part // 2) + at) * half
        term = contract(
            slots[pl.ds(start, rows), lane : lane + half],
            w[:, part * width : (part + 1) * width],
            1,
            0,
        )
        total = term if total is None else total + term
    return total


def sibling_kernel(where, slots, w0, w1, w2, w3, out):
    quads, cap, width = out.shape[0], out.shape[1], w0.shape[1] // 3
    for part in range(3):
        total = partial_sum(slots, (w0, w1, w2, w3), 1 - where[0], quads * cap, part)
        for quad in range(quads):
            out[quad, :, part * width : (part + 1) * width] = total[
                quad * cap : (quad + 1) * cap
            ].astype(out.dtype)


def split_kernel(
    where, slots, w0, w1, w2, w3, other, far_right, far_left, own, ahead, behind, mine
):
    quads, cap, width = other.shape[0], other.shape[1], w0.shape[1] // 3
    core, me, cut = where[0], where[1], far_right.shape[1]
    for part in range(3):
        lanes = slice(part * width, (part + 1) * width)
        total = partial_sum(slots, (w0, w1, w2, w3), core, quads * cap, part)
        for quad in range(quads):
            mine[quad, :, lanes] = total[quad * cap : (quad + 1) * cap] + other[
                quad, :, lanes
            ].astype(F32)

    def piece(step, lanes):
        return mine[jnp.bitwise_and(me + step, QUAD - 1), :, lanes]

    whole = slice(0, 2 * cut)
    far_right[...] = piece(2, slice(0, cut)).astype(BF)
    far_left[...] = piece(2, slice(cut, 2 * cut)).astype(BF)
    own[...] = piece(0, whole)
    ahead[...] = piece(1, whole)
    behind[...] = piece(3, whole)


def relay_kernel(ahead, behind, from_left, from_right, to_right, to_left):
    cut = from_left.shape[1]
    to_right[:, :cut] = (ahead[:, :cut] + from_left[...].astype(F32)).astype(BF)
    to_right[:, cut:] = ahead[:, cut:].astype(BF)
    to_left[:, :cut] = behind[:, :cut].astype(BF)
    to_left[:, cut:] = (behind[:, cut:] + from_right[...].astype(F32)).astype(BF)


def activate_kernel(own, from_left, from_right, out):
    width = own.shape[1] // 3

    def total(start):
        lanes = slice(start, start + width)
        return own[:, lanes] + from_left[:, lanes].astype(F32) + from_right[:, lanes].astype(F32)

    gate_val, up_val, back_hidden = total(0), total(width), total(2 * width)
    sigmoid_gate = jax.nn.sigmoid(gate_val)
    active = gate_val * sigmoid_gate
    out[:, :width] = (
        back_hidden * up_val * sigmoid_gate * (1.0 + gate_val * (1.0 - sigmoid_gate))
    ).astype(BF)
    out[:, width : 2 * width] = (back_hidden * active).astype(BF)
    out[:, 2 * width :] = (active * up_val).astype(BF)


def outs_kernel(rows, w0, w1, w2, w3, out):
    width, half = w0.shape[1] // 3, w0.shape[0]
    for at, w in enumerate((w0, w1, w2, w3)):
        value = contract(rows[:, 2 * width :], w[:, 2 * width :], 1, 1)
        out[:, at * half : (at + 1) * half] = value.astype(BF)
        value = contract(rows[:, : 2 * width], w[:, : 2 * width], 1, 1)
        out[:, (4 + at) * half : (5 + at) * half] = value.astype(BF)


def grads_kernel(slots, rows, after, g0, g1, g2, g3):
    del after
    width, half = g0.shape[1] // 3, g0.shape[0]
    for at, g in enumerate((g0, g1, g2, g3)):
        left = slots[:, at * half : (at + 1) * half]
        value = contract(left, rows[:, : 2 * width], 0, 0)
        g[:, : 2 * width] = value.astype(g.dtype)
        left = slots[:, (4 + at) * half : (5 + at) * half]
        value = contract(left, rows[:, 2 * width :], 0, 0)
        g[:, 2 * width :] = value.astype(g.dtype)


def combine_kernel(route, weight, home, mixed, grad):
    experts, cap, feats = home.shape[0], home.shape[1], mixed.shape[1]
    one, two = place_routes(route[...], experts, cap)
    slots = jnp.concatenate([home[e].astype(F32) for e in range(experts)], axis=0).astype(BF)
    mixed[...] = (
        weight[:, 0:1] * contract(one, slots[:, :feats], 1, 0)
        + weight[:, 1:2] * contract(two, slots[:, :feats], 1, 0)
    ).astype(BF)
    grad[...] = contract(one + two, slots[:, feats:], 1, 0).astype(BF)


def finish_kernel(g0, g1, g2, g3, ng, nu, nd, mg, sg, mu, su, md, sd):
    width = ng.shape[2]

    def total(start):
        lanes = slice(start, start + width)
        return (g0[:, lanes] + g1[:, lanes].astype(F32)) + (
            g2[:, lanes].astype(F32) + g3[:, lanes].astype(F32)
        )

    gate = total(0)
    mg[0] = gate
    sg[0] = gate * ng[0].astype(F32)
    up = total(width)
    mu[0] = up
    su[0] = up * nu[0].astype(F32)
    down = total(2 * width).T
    md[0] = down
    sd[0] = down * nd[0].astype(F32)


def ones_where(condition):
    return jnp.where(condition, 1.0, 0.0).astype(F32)


def place_routes(route, experts, capacity):
    rows = route.shape[0]
    names = lax.broadcasted_iota(jnp.int32, (rows, experts), 1)
    first = ones_where(route[:, 0:1] == names)
    second = ones_where(route[:, 1:2] == names)
    below = ones_where(
        lax.broadcasted_iota(jnp.int32, (rows, rows), 0)
        > lax.broadcasted_iota(jnp.int32, (rows, rows), 1)
    ).astype(BF)
    earlier = contract(below, (first + second).astype(BF), 1, 0)
    place_first = jnp.sum(earlier * first, axis=1, keepdims=True).astype(jnp.int32)
    place_second = jnp.sum((earlier + first) * second, axis=1, keepdims=True).astype(jnp.int32)
    slots = lax.broadcasted_iota(jnp.int32, (rows, experts * capacity), 1)
    one = ones_where(route[:, 0:1] * capacity + place_first == slots).astype(BF)
    two = ones_where(route[:, 1:2] * capacity + place_second == slots).astype(BF)
    return one, two


def body(
    tokens,
    cotangent,
    route,
    route_weight,
    mean_gate,
    spread_gate,
    noise_gate,
    mean_up,
    spread_up,
    noise_up,
    mean_down,
    spread_down,
    noise_down,
):
    experts = lax.axis_size(PLANE)
    group_rows, routes = route.shape
    feats = tokens.shape[1]
    half = feats // 2
    width = mean_gate.shape[2]
    cap = group_rows * routes // experts * 3 // 2
    rows_all = 2 * QUAD * cap
    me = lax.axis_index("za").astype(jnp.int32).reshape(1)
    zb = lax.axis_index("zb").astype(jnp.int32).reshape(1)
    core = lax.axis_index("core").astype(jnp.int32).reshape(1)

    w_own = pl.pallas_call(
        sample_kernel,
        out_shape=jax.ShapeDtypeStruct((half, 3 * width), BF),
        in_specs=[pl.BlockSpec(memory_space=pltpu.HBM)] * 9,
        out_specs=pl.BlockSpec(memory_space=pltpu.VMEM),
        scratch_shapes=[
            pltpu.VMEM((6, half, width), BF),
            pltpu.VMEM((3, width, half), BF),
            pltpu.SemaphoreType.DMA((9,)),
        ],
        compiler_params=pltpu.CompilerParams(vmem_limit_bytes=60 * 1024 * 1024),
    )(
        mean_gate,
        spread_gate,
        noise_gate,
        mean_up,
        spread_up,
        noise_up,
        mean_down,
        spread_down,
        noise_down,
    )
    weights = (
        w_own,
        along_ring(w_own, (-1, -1)),
        along_ring(w_own, (1, 1)),
        along_ring(w_own, (-2, 2)),
    )

    (send,) = kernel_call(
        pick_kernel,
        [jax.ShapeDtypeStruct((experts, cap, 2 * feats), BF)],
        route,
        route_weight,
        tokens,
        cotangent,
    )
    got = lax.all_to_all(send, PLANE, split_axis=0, concat_axis=0, tiled=True)
    (got,) = kernel_call(
        spread_kernel,
        [jax.ShapeDtypeStruct((2 * QUAD, cap, 8 * half), BF)],
        zb,
        got,
        *weights[1:],
        scalars=1,
        free=3,
    )
    got = lax.all_to_all(got, ("core", "za"), split_axis=0, concat_axis=0, tiled=True)
    slots = got.reshape(rows_all, 8 * half)

    (other,) = kernel_call(
        sibling_kernel,
        [jax.ShapeDtypeStruct((QUAD, cap, 3 * width), BF)],
        core,
        slots,
        *weights,
        scalars=1,
    )
    other = lax.ppermute(other, "core", [(0, 1), (1, 0)])
    cut = 3 * width // 2
    total = jax.ShapeDtypeStruct((cap, 3 * width), F32)
    wire = jax.ShapeDtypeStruct((cap, 3 * width), BF)
    half_wire = jax.ShapeDtypeStruct((cap, cut), BF)
    far_right, far_left, own, ahead, behind = kernel_call(
        split_kernel,
        [half_wire] * 2 + [total] * 3,
        jnp.concatenate([core, me]),
        slots,
        *weights,
        other,
        scalars=1,
        scratch=[pltpu.VMEM((QUAD, cap, 3 * width), F32)],
    )
    to_right, to_left = kernel_call(
        relay_kernel, [wire] * 2, ahead, behind, shift(far_right, 1), shift(far_left, -1)
    )
    (rows,) = kernel_call(
        activate_kernel, [wire], own, shift(to_right, 1), shift(to_left, -1)
    )

    rows = lax.all_gather(rows, "za", axis=0, tiled=True)
    rows = lax.all_gather(rows, "core", axis=0, tiled=True)
    (outs,) = kernel_call(
        outs_kernel, [jax.ShapeDtypeStruct((rows_all, 8 * half), BF)], rows, *weights
    )
    outs = outs.reshape(2 * QUAD, cap, 8 * half)
    home = lax.all_to_all(outs, ("core", "za"), split_axis=0, concat_axis=0, tiled=True)

    w_sent = kernel_call(
        grads_kernel,
        [jax.ShapeDtypeStruct((half, 3 * width), F32)]
        + [jax.ShapeDtypeStruct((half, 3 * width), BF)] * 3,
        slots,
        rows,
        home,
        free=1,
    )
    w_grads = (
        w_sent[0],
        along_ring(w_sent[1], (1, 1)),
        along_ring(w_sent[2], (-1, -1)),
        along_ring(w_sent[3], (2, -2)),
    )

    (home,) = kernel_call(
        collect_kernel,
        [jax.ShapeDtypeStruct((experts, cap, 2 * feats), BF)],
        zb,
        home,
        w_sent[3],
        scalars=1,
        free=1,
    )
    home = lax.all_to_all(home, PLANE, split_axis=0, concat_axis=0, tiled=True)
    mixed_out, token_grad = kernel_call(
        combine_kernel,
        [jax.ShapeDtypeStruct((group_rows, feats), BF)] * 2,
        route,
        route_weight,
        home,
    )
    by_row = jax.ShapeDtypeStruct((1, half, width), F32)
    by_column = jax.ShapeDtypeStruct((1, width, half), F32)
    ends = kernel_call(
        finish_kernel,
        [by_row] * 4 + [by_column] * 2,
        *w_grads,
        noise_gate,
        noise_up,
        noise_down,
    )
    return (mixed_out, token_grad) + tuple(ends)


def solution(mesh):
    fine = Mesh(mesh.devices.reshape(4, 4, QUAD, 4, 2), PLANE + RING)
    by_token = P(RING, PLANE)
    by_group = P(RING, None)
    by_row = P(PLANE, RING, None)
    by_column = P(PLANE, None, RING)
    return jax.shard_map(
        body,
        mesh=fine,
        in_specs=(by_token,) * 2 + (by_group,) * 2 + (by_row,) * 6 + (by_column,) * 3,
        out_specs=(by_token,) * 2 + (by_row,) * 4 + (by_column,) * 2,
        check_vma=False,
    )
```

```python
import itertools

import jax
import jax.numpy as jnp
from jax import lax
from jax.experimental import pallas as pl
from jax.experimental.pallas import tpu as pltpu
from jax.sharding import Mesh, PartitionSpec as P

BF = jnp.bfloat16
F32 = jnp.float32
PLANE = ("y", "x")
RING = ("za", "zb", "core")
QUAD = 4
NOTES = 16
WINDOW = ((0, 1, -1, 2), (0, 1, -1, -2))


def sampled(mean_part, spread, noise_part):
    return (mean_part.astype(F32) + spread.astype(F32) * noise_part.astype(F32)).astype(BF)


def contract(left_side, right_side, left_dim, right_dim):
    return lax.dot_general(
        left_side,
        right_side,
        (((left_dim,), (right_dim,)), ((), ())),
        preferred_element_type=F32,
    )


def shift(value, step):
    return lax.ppermute(value, "za", [(i, (i + step) % QUAD) for i in range(QUAD)])


def along_ring(value, steps):
    chips = lax.axis_size("za") * lax.axis_size("zb")
    pairs = [
        (2 * z + core, 2 * ((z + steps[core]) % chips) + core)
        for z in range(chips)
        for core in range(2)
    ]
    return lax.ppermute(value, RING, pairs)


def to_window(value, cross, back=False):
    sizes = [lax.axis_size(name) for name in PLANE + RING]
    quads = sizes[3]

    def index(place):
        number = 0
        for size, at in zip(sizes, place):
            number = number * size + at
        return number

    pairs = []
    for y, x, za, zb, core in itertools.product(*map(range, sizes)):
        side = 1 - core if cross else core
        for goal in range(QUAD):
            for step in WINDOW[side]:
                if (quads * goal + zb + step - quads * y - x) % (QUAD * quads) == 0:
                    pair = (index((y, x, za, zb, core)), index((za, x, goal, zb, side)))
                    pairs.append(pair[::-1] if back else pair)
    return lax.ppermute(value, PLANE + RING, pairs)


def kernel_call(kernel, outs, *operands, free=0, scalars=0, scratch=()):
    whole = pl.BlockSpec(memory_space=pltpu.VMEM)
    count = len(operands) - free - scalars
    moved = sum(a.size * a.dtype.itemsize for a in operands) + sum(
        o.size * o.dtype.itemsize for o in outs
    )
    return pl.pallas_call(
        kernel,
        out_shape=tuple(outs),
        in_specs=[pl.BlockSpec(memory_space=pltpu.SMEM)] * scalars
        + [whole] * count
        + [pl.BlockSpec(memory_space=pl.ANY)] * free,
        out_specs=(whole,) * len(outs),
        scratch_shapes=list(scratch),
        compiler_params=pltpu.CompilerParams(vmem_limit_bytes=8 * 1024 * 1024),
        cost_estimate=pl.CostEstimate(flops=0, bytes_accessed=moved, transcendentals=0),
    )(*operands)


def sample_kernel(*refs):
    sources, (out, rows, columns, done) = refs[:9], refs[-4:]
    places = [rows.at[i] for i in range(6)] + [columns.at[i] for i in range(3)]
    copies = [
        pltpu.make_async_copy(source.at[0], place, done.at[i])
        for i, (source, place) in enumerate(zip(sources, places))
    ]
    for copy in copies:
        copy.start()
    width = rows.shape[2]
    for part in range(2):
        for copy in copies[3 * part : 3 * part + 3]:
            copy.wait()
        out[:, part * width : (part + 1) * width] = sampled(
            rows[3 * part], rows[3 * part + 1], rows[3 * part + 2]
        )
    for copy in copies[6:]:
        copy.wait()
    down = columns[0].astype(F32) + columns[1].astype(F32) * columns[2].astype(F32)
    out[:, 2 * width :] = down.T.astype(BF)


def pack_kernel(where, route, weight, tokens, cotangent, same, cross):
    rows, half = tokens.shape[0], tokens.shape[1] // 2
    experts = 2 * 2 * QUAD
    columns = place_routes(route[...], experts)
    for r in range(2):
        rest = weight[:, r : r + 1]
        for _ in range(3):
            term = rest.astype(BF).astype(F32)
            columns.append(term)
            rest = rest - term
    names = lax.broadcasted_iota(jnp.int32, (rows, rows), 1)
    table = jnp.zeros((rows, rows), F32)
    for at, column in enumerate(columns):
        table = jnp.where(names == at, column, table)
    table = table.T[:NOTES].astype(BF)
    core = where[0]
    for out, side in ((same, core), (cross, 1 - core)):
        for kind, source in enumerate((tokens, cotangent)):
            lanes = slice(kind * half, (kind + 1) * half)
            out[:rows, lanes] = jnp.where(side == 0, source[:, :half], source[:, half:])
            out[rows:, lanes] = table[:, :half]


def selection(packed, slots):
    rows = packed.shape[0] - NOTES
    notes = packed[rows:, :rows].astype(F32)
    names = lax.broadcasted_iota(jnp.int32, (slots, rows), 0)
    chosen, weights = [], []
    for r in range(2):
        cap = slots // (4 * QUAD)
        target = (notes[r : r + 1] * cap + notes[2 + r : 3 + r]).astype(jnp.int32)
        chosen.append(ones_where(target == names))
        at = 4 + 3 * r
        weights.append((notes[at : at + 1] + notes[at + 1 : at + 2]) + notes[at + 2 : at + 3])
    return chosen, weights


def pick_kernel(where, same, cross, out):
    experts, cap, half = out.shape[0], out.shape[2], out.shape[3] // 2
    rows = same.shape[0] - NOTES
    for packed, side in ((same, where[0]), (cross, 1 - where[0])):
        chosen, weights = selection(packed, experts * cap)
        both = (chosen[0] + chosen[1]).astype(BF)
        weight = jnp.sum(
            chosen[0] * weights[0] + chosen[1] * weights[1], axis=1, keepdims=True
        )
        x = contract(both, packed[:rows, :half], 1, 0)
        d = weight * contract(both, packed[:rows, half:], 1, 0)
        for expert in range(experts):
            at = slice(expert * cap, (expert + 1) * cap)
            out[expert, side, :, :half] = x[at].astype(BF)
            out[expert, side, :, half:] = d[at].astype(BF)


def spread_kernel(where, got, out):
    half = got.shape[3] // 2
    for za in range(QUAD):
        for at, step in enumerate(WINDOW[0]):
            chip = 4 * za + jnp.bitwise_and(where[0] + (step + 4), 3)
            for core in range(2):
                for kind in range(2):
                    lane = (4 * kind + at) * half
                    out[core * QUAD + za, :, lane : lane + half] = got[
                        chip, core, :, kind * half : (kind + 1) * half
                    ]


def collect_kernel(where, got, *rest):
    out = rest[-1]
    half = out.shape[3] // 2
    for za in range(QUAD):
        for at, step in enumerate(WINDOW[0]):
            chip = 4 * za + jnp.bitwise_and(where[0] + (step + 4), 3)
            for core in range(2):
                for kind in range(2):
                    lane = (4 * kind + at) * half
                    out[chip, core, :, kind * half : (kind + 1) * half] = got[
                        core * QUAD + za, :, lane : lane + half
                    ]


def combine_kernel(where, same, cross, home, to_same, to_cross):
    experts, cap, half = home.shape[0], home.shape[2], home.shape[3] // 2
    for packed, side, out in (
        (same, where[0], to_same),
        (cross, 1 - where[0], to_cross),
    ):
        rows = out.shape[0]
        chosen, weights = selection(packed, experts * cap)
        columns = jnp.concatenate(weights * 4, axis=0).T
        slots = jnp.concatenate(
            [home[expert, side].astype(F32) for expert in range(experts)], axis=0
        ).astype(BF)
        one, two = chosen[0].astype(BF), chosen[1].astype(BF)
        out[:, :half] = (
            columns[:, 0:1] * contract(one, slots[:, :half], 0, 0)
            + columns[:, 1:2] * contract(two, slots[:, :half], 0, 0)
        ).astype(BF)
        out[:, half:] = contract(one + two, slots[:, half:], 0, 0).astype(BF)


def unpack_kernel(where, same, cross, mixed, grad):
    half = same.shape[1] // 2
    first = where[0] == 0
    for kind, out in enumerate((mixed, grad)):
        lanes = slice(kind * half, (kind + 1) * half)
        out[:, :half] = jnp.where(first, same[:, lanes], cross[:, lanes])
        out[:, half:] = jnp.where(first, cross[:, lanes], same[:, lanes])


def partial_sum(slots, weights, side, rows, part):
    width, half = weights[0].shape[1] // 3, weights[0].shape[0]
    start = pl.multiple_of(side * rows, rows)
    total = None
    for at, w in enumerate(weights):
        lane = (4 * (part // 2) + at) * half
        term = contract(
            slots[pl.ds(start, rows), lane : lane + half],
            w[:, part * width : (part + 1) * width],
            1,
            0,
        )
        total = term if total is None else total + term
    return total


def sibling_kernel(where, slots, w0, w1, w2, w3, out):
    quads, cap, width = out.shape[0], out.shape[1], w0.shape[1] // 3
    for part in range(3):
        total = partial_sum(slots, (w0, w1, w2, w3), 1 - where[0], quads * cap, part)
        for quad in range(quads):
            out[quad, :, part * width : (part + 1) * width] = total[
                quad * cap : (quad + 1) * cap
            ].astype(out.dtype)


def split_kernel(
    where, slots, w0, w1, w2, w3, other, far_right, far_left, own, ahead, behind, mine
):
    quads, cap, width = other.shape[0], other.shape[1], w0.shape[1] // 3
    core, me, cut = where[0], where[1], far_right.shape[1]
    for part in range(3):
        lanes = slice(part * width, (part + 1) * width)
        total = partial_sum(slots, (w0, w1, w2, w3), core, quads * cap, part)
        for quad in range(quads):
            mine[quad, :, lanes] = total[quad * cap : (quad + 1) * cap] + other[
                quad, :, lanes
            ].astype(F32)

    def piece(step, lanes):
        return mine[jnp.bitwise_and(me + step, QUAD - 1), :, lanes]

    whole = slice(0, 2 * cut)
    far_right[...] = piece(2, slice(0, cut)).astype(BF)
    far_left[...] = piece(2, slice(cut, 2 * cut)).astype(BF)
    own[...] = piece(0, whole)
    ahead[...] = piece(1, whole)
    behind[...] = piece(3, whole)


def relay_kernel(ahead, behind, from_left, from_right, to_right, to_left):
    cut = from_left.shape[1]
    to_right[:, :cut] = (ahead[:, :cut] + from_left[...].astype(F32)).astype(BF)
    to_right[:, cut:] = ahead[:, cut:].astype(BF)
    to_left[:, :cut] = behind[:, :cut].astype(BF)
    to_left[:, cut:] = (behind[:, cut:] + from_right[...].astype(F32)).astype(BF)


def activate_kernel(own, from_left, from_right, out):
    width = own.shape[1] // 3

    def total(start):
        lanes = slice(start, start + width)
        return own[:, lanes] + from_left[:, lanes].astype(F32) + from_right[:, lanes].astype(F32)

    gate_val, up_val, back_hidden = total(0), total(width), total(2 * width)
    sigmoid_gate = jax.nn.sigmoid(gate_val)
    active = gate_val * sigmoid_gate
    out[:, :width] = (
        back_hidden * up_val * sigmoid_gate * (1.0 + gate_val * (1.0 - sigmoid_gate))
    ).astype(BF)
    out[:, width : 2 * width] = (back_hidden * active).astype(BF)
    out[:, 2 * width :] = (active * up_val).astype(BF)


def outs_kernel(rows, w0, w1, w2, w3, out):
    width, half = w0.shape[1] // 3, w0.shape[0]
    for at, w in enumerate((w0, w1, w2, w3)):
        value = contract(rows[:, 2 * width :], w[:, 2 * width :], 1, 1)
        out[:, at * half : (at + 1) * half] = value.astype(BF)
        value = contract(rows[:, : 2 * width], w[:, : 2 * width], 1, 1)
        out[:, (4 + at) * half : (5 + at) * half] = value.astype(BF)


def grads_kernel(slots, rows, g0, g1, g2, g3):
    width, half = g0.shape[1] // 3, g0.shape[0]
    for at, g in enumerate((g0, g1, g2, g3)):
        left = slots[:, at * half : (at + 1) * half]
        value = contract(left, rows[:, : 2 * width], 0, 0)
        g[:, : 2 * width] = value.astype(g.dtype)
        left = slots[:, (4 + at) * half : (5 + at) * half]
        value = contract(left, rows[:, 2 * width :], 0, 0)
        g[:, 2 * width :] = value.astype(g.dtype)


def finish_kernel(g0, g1, g2, g3, ng, nu, nd, mg, sg, mu, su, md, sd):
    width = ng.shape[2]

    def total(start):
        lanes = slice(start, start + width)
        return (g0[:, lanes] + g1[:, lanes].astype(F32)) + (
            g2[:, lanes].astype(F32) + g3[:, lanes].astype(F32)
        )

    gate = total(0)
    mg[0] = gate
    sg[0] = gate * ng[0].astype(F32)
    up = total(width)
    mu[0] = up
    su[0] = up * nu[0].astype(F32)
    down = total(2 * width).T
    md[0] = down
    sd[0] = down * nd[0].astype(F32)


def ones_where(condition):
    return jnp.where(condition, 1.0, 0.0).astype(F32)


def place_routes(route, experts):
    rows = route.shape[0]
    names = lax.broadcasted_iota(jnp.int32, (rows, experts), 1)
    first = ones_where(route[:, 0:1] == names)
    second = ones_where(route[:, 1:2] == names)
    below = ones_where(
        lax.broadcasted_iota(jnp.int32, (rows, rows), 0)
        > lax.broadcasted_iota(jnp.int32, (rows, rows), 1)
    ).astype(BF)
    earlier = contract(below, (first + second).astype(BF), 1, 0)
    return [
        route[:, 0:1].astype(F32),
        route[:, 1:2].astype(F32),
        jnp.sum(earlier * first, axis=1, keepdims=True),
        jnp.sum((earlier + first) * second, axis=1, keepdims=True),
    ]


def body(
    tokens,
    cotangent,
    route,
    route_weight,
    mean_gate,
    spread_gate,
    noise_gate,
    mean_up,
    spread_up,
    noise_up,
    mean_down,
    spread_down,
    noise_down,
):
    experts = lax.axis_size(PLANE)
    group_rows, routes = route.shape
    feats = tokens.shape[1]
    half = feats // 2
    width = mean_gate.shape[2]
    cap = group_rows * routes // experts * 3 // 2
    rows_all = 2 * QUAD * cap
    me = lax.axis_index("za").astype(jnp.int32).reshape(1)
    zb = lax.axis_index("zb").astype(jnp.int32).reshape(1)
    core = lax.axis_index("core").astype(jnp.int32).reshape(1)

    packed = kernel_call(
        pack_kernel,
        [jax.ShapeDtypeStruct((group_rows + NOTES, 2 * half), BF)] * 2,
        core,
        route,
        route_weight,
        tokens,
        cotangent,
        scalars=1,
    )
    same = to_window(packed[0], False)
    cross = to_window(packed[1], True)
    w_own = pl.pallas_call(
        sample_kernel,
        out_shape=jax.ShapeDtypeStruct((half, 3 * width), BF),
        in_specs=[pl.BlockSpec(memory_space=pltpu.HBM)] * 9
        + [pl.BlockSpec(memory_space=pl.ANY)] * 2,
        out_specs=pl.BlockSpec(memory_space=pltpu.VMEM),
        scratch_shapes=[
            pltpu.VMEM((6, half, width), BF),
            pltpu.VMEM((3, width, half), BF),
            pltpu.SemaphoreType.DMA((9,)),
        ],
        compiler_params=pltpu.CompilerParams(vmem_limit_bytes=60 * 1024 * 1024),
    )(
        mean_gate,
        spread_gate,
        noise_gate,
        mean_up,
        spread_up,
        noise_up,
        mean_down,
        spread_down,
        noise_down,
        same,
        cross,
    )
    weights = (
        w_own,
        along_ring(w_own, (-1, -1)),
        along_ring(w_own, (1, 1)),
        along_ring(w_own, (-2, 2)),
    )

    (send,) = kernel_call(
        pick_kernel,
        [jax.ShapeDtypeStruct((experts, 2, cap, 2 * half), BF)],
        core,
        same,
        cross,
        scalars=1,
    )
    got = lax.all_to_all(send, PLANE, split_axis=0, concat_axis=0, tiled=True)
    (got,) = kernel_call(
        spread_kernel,
        [jax.ShapeDtypeStruct((2 * QUAD, cap, 8 * half), BF)],
        zb,
        got,
        scalars=1,
    )
    slots = got.reshape(rows_all, 8 * half)

    (other,) = kernel_call(
        sibling_kernel,
        [jax.ShapeDtypeStruct((QUAD, cap, 3 * width), BF)],
        core,
        slots,
        *weights,
        scalars=1,
    )
    other = lax.ppermute(other, "core", [(0, 1), (1, 0)])
    cut = 3 * width // 2
    total = jax.ShapeDtypeStruct((cap, 3 * width), F32)
    wire = jax.ShapeDtypeStruct((cap, 3 * width), BF)
    half_wire = jax.ShapeDtypeStruct((cap, cut), BF)
    far_right, far_left, own, ahead, behind = kernel_call(
        split_kernel,
        [half_wire] * 2 + [total] * 3,
        jnp.concatenate([core, me]),
        slots,
        *weights,
        other,
        scalars=1,
        scratch=[pltpu.VMEM((QUAD, cap, 3 * width), F32)],
    )
    to_right, to_left = kernel_call(
        relay_kernel, [wire] * 2, ahead, behind, shift(far_right, 1), shift(far_left, -1)
    )
    (rows,) = kernel_call(
        activate_kernel, [wire], own, shift(to_right, 1), shift(to_left, -1)
    )

    rows = lax.all_gather(rows, "za", axis=0, tiled=True)
    rows = lax.all_gather(rows, "core", axis=0, tiled=True)
    (outs,) = kernel_call(
        outs_kernel, [jax.ShapeDtypeStruct((rows_all, 8 * half), BF)], rows, *weights
    )
    outs = outs.reshape(2 * QUAD, cap, 8 * half)
    w_sent = kernel_call(
        grads_kernel,
        [jax.ShapeDtypeStruct((half, 3 * width), F32)]
        + [jax.ShapeDtypeStruct((half, 3 * width), BF)] * 3,
        slots,
        rows,
    )
    w_grads = (
        w_sent[0],
        along_ring(w_sent[1], (1, 1)),
        along_ring(w_sent[2], (-1, -1)),
        along_ring(w_sent[3], (2, -2)),
    )

    (home,) = kernel_call(
        collect_kernel,
        [jax.ShapeDtypeStruct((experts, 2, cap, 2 * half), BF)],
        zb,
        outs,
        w_sent[3],
        scalars=1,
        free=1,
    )
    home = lax.all_to_all(home, PLANE, split_axis=0, concat_axis=0, tiled=True)
    ready = kernel_call(
        combine_kernel,
        [jax.ShapeDtypeStruct((group_rows, 2 * half), BF)] * 2,
        core,
        same,
        cross,
        home,
        scalars=1,
    )
    mixed_out, token_grad = kernel_call(
        unpack_kernel,
        [jax.ShapeDtypeStruct((group_rows, feats), BF)] * 2,
        core,
        to_window(ready[0], False, True),
        to_window(ready[1], True, True),
        scalars=1,
    )
    by_row = jax.ShapeDtypeStruct((1, half, width), F32)
    by_column = jax.ShapeDtypeStruct((1, width, half), F32)
    ends = kernel_call(
        finish_kernel,
        [by_row] * 4 + [by_column] * 2,
        *w_grads,
        noise_gate,
        noise_up,
        noise_down,
    )
    return (mixed_out, token_grad) + tuple(ends)


def solution(mesh):
    fine = Mesh(mesh.devices.reshape(4, 4, QUAD, 4, 2), PLANE + RING)
    by_token = P(RING, PLANE)
    by_group = P(RING, None)
    by_row = P(PLANE, RING, None)
    by_column = P(PLANE, None, RING)
    return jax.shard_map(
        body,
        mesh=fine,
        in_specs=(by_token,) * 2 + (by_group,) * 2 + (by_row,) * 6 + (by_column,) * 3,
        out_specs=(by_token,) * 2 + (by_row,) * 4 + (by_column,) * 2,
        check_vma=False,
    )
```

```python
import itertools

import jax
import jax.numpy as jnp
from jax import lax
from jax.experimental import pallas as pl
from jax.experimental.pallas import tpu as pltpu
from jax.sharding import Mesh, PartitionSpec as P

BF = jnp.bfloat16
F32 = jnp.float32
PLANE = ("y", "x")
RING = ("za", "zb", "core")
QUAD = 4
NOTES = 16
WINDOW = ((0, 1, -1, 2), (0, 1, -1, -2))


def sampled(mean_part, spread, noise_part):
    return (mean_part.astype(F32) + spread.astype(F32) * noise_part.astype(F32)).astype(BF)


def contract(left_side, right_side, left_dim, right_dim):
    return lax.dot_general(
        left_side,
        right_side,
        (((left_dim,), (right_dim,)), ((), ())),
        preferred_element_type=F32,
    )


def shift(value, step):
    return lax.ppermute(value, "za", [(i, (i + step) % QUAD) for i in range(QUAD)])


def along_ring(value, steps):
    chips = lax.axis_size("za") * lax.axis_size("zb")
    pairs = [
        (2 * z + core, 2 * ((z + steps[core]) % chips) + core)
        for z in range(chips)
        for core in range(2)
    ]
    return lax.ppermute(value, RING, pairs)


def to_window(value, cross, back=False):
    sizes = [lax.axis_size(name) for name in PLANE + RING]
    quads = sizes[3]

    def index(place):
        number = 0
        for size, at in zip(sizes, place):
            number = number * size + at
        return number

    pairs = []
    for y, x, za, zb, core in itertools.product(*map(range, sizes)):
        side = 1 - core if cross else core
        for goal in range(QUAD):
            for step in WINDOW[side]:
                if (quads * goal + zb + step - quads * y - x) % (QUAD * quads) == 0:
                    pair = (
                        index((y, x, za, zb, core)),
                        index(((za + goal) % QUAD, x, goal, zb, side)),
                    )
                    pairs.append(pair[::-1] if back else pair)
    return lax.ppermute(value, PLANE + RING, pairs)


def kernel_call(kernel, outs, *operands, free=0, scalars=0, scratch=()):
    whole = pl.BlockSpec(memory_space=pltpu.VMEM)
    count = len(operands) - free - scalars
    moved = sum(a.size * a.dtype.itemsize for a in operands) + sum(
        o.size * o.dtype.itemsize for o in outs
    )
    return pl.pallas_call(
        kernel,
        out_shape=tuple(outs),
        in_specs=[pl.BlockSpec(memory_space=pltpu.SMEM)] * scalars
        + [whole] * count
        + [pl.BlockSpec(memory_space=pl.ANY)] * free,
        out_specs=(whole,) * len(outs),
        scratch_shapes=list(scratch),
        compiler_params=pltpu.CompilerParams(vmem_limit_bytes=8 * 1024 * 1024),
        cost_estimate=pl.CostEstimate(flops=0, bytes_accessed=moved, transcendentals=0),
    )(*operands)


def sample_kernel(*refs):
    sources, (out, rows, columns, done) = refs[:9], refs[-4:]
    places = [rows.at[i] for i in range(6)] + [columns.at[i] for i in range(3)]
    copies = [
        pltpu.make_async_copy(source.at[0], place, done.at[i])
        for i, (source, place) in enumerate(zip(sources, places))
    ]
    for copy in copies:
        copy.start()
    width = rows.shape[2]
    for part in range(2):
        for copy in copies[3 * part : 3 * part + 3]:
            copy.wait()
        out[:, part * width : (part + 1) * width] = sampled(
            rows[3 * part], rows[3 * part + 1], rows[3 * part + 2]
        )
    for copy in copies[6:]:
        copy.wait()
    down = columns[0].astype(F32) + columns[1].astype(F32) * columns[2].astype(F32)
    out[:, 2 * width :] = down.T.astype(BF)


def pack_kernel(where, *refs):
    sources, (same, cross), places, done = refs[:4], refs[4:6], refs[6:10], refs[10]
    copies = [
        pltpu.make_async_copy(source, place, done.at[i])
        for i, (source, place) in enumerate(zip(sources, places))
    ]
    for copy in copies:
        copy.start()
    for copy in copies:
        copy.wait()
    route, weight, tokens, cotangent = places
    rows, half = tokens.shape[0], tokens.shape[1] // 2
    notes = place_routes(route[...], 4 * QUAD)
    for r in range(2):
        rest = weight[r : r + 1]
        for _ in range(3):
            term = rest.astype(BF).astype(F32)
            notes.append(term)
            rest = rest - term
    notes.append(jnp.zeros((NOTES - len(notes), rows), F32))
    table = jnp.concatenate(notes, axis=0).astype(BF)
    core = where[0]
    for out, side in ((same, core), (cross, 1 - core)):
        for kind, source in enumerate((tokens, cotangent)):
            lanes = slice(kind * half, (kind + 1) * half)
            out[:rows, lanes] = jnp.where(side == 0, source[:, :half], source[:, half:])
            out[rows:, lanes] = table[:, :half]


def selection(packed, slots):
    rows = packed.shape[0] - NOTES
    notes = packed[rows:, :rows].astype(F32)
    names = lax.broadcasted_iota(jnp.int32, (slots, rows), 0)
    chosen, weights = [], []
    for r in range(2):
        cap = slots // (4 * QUAD)
        target = (notes[r : r + 1] * cap + notes[2 + r : 3 + r]).astype(jnp.int32)
        chosen.append(ones_where(target == names))
        at = 4 + 3 * r
        weights.append((notes[at : at + 1] + notes[at + 1 : at + 2]) + notes[at + 2 : at + 3])
    return chosen, weights


def pick_kernel(where, same, cross, out):
    experts, cap, half = out.shape[0], out.shape[2], out.shape[3] // 2
    rows = same.shape[0] - NOTES
    for packed, side in ((same, where[0]), (cross, 1 - where[0])):
        chosen, weights = selection(packed, experts * cap)
        both = (chosen[0] + chosen[1]).astype(BF)
        weight = jnp.sum(
            chosen[0] * weights[0] + chosen[1] * weights[1], axis=1, keepdims=True
        )
        x = contract(both, packed[:rows, :half], 1, 0)
        d = weight * contract(both, packed[:rows, half:], 1, 0)
        for expert in range(experts):
            at = slice(expert * cap, (expert + 1) * cap)
            out[expert, side, :, :half] = x[at].astype(BF)
            out[expert, side, :, half:] = d[at].astype(BF)


def spread_kernel(where, got, out):
    half = got.shape[3] // 2
    for za in range(QUAD):
        for at, step in enumerate(WINDOW[0]):
            chip = 4 * jnp.bitwise_and(where[1] + za, 3) + jnp.bitwise_and(where[0] + (step + 4), 3)
            for core in range(2):
                for kind in range(2):
                    lane = (4 * kind + at) * half
                    out[core * QUAD + za, :, lane : lane + half] = got[
                        chip, core, :, kind * half : (kind + 1) * half
                    ]


def collect_kernel(where, got, *rest):
    out = rest[-1]
    half = out.shape[3] // 2
    for za in range(QUAD):
        for at, step in enumerate(WINDOW[0]):
            chip = 4 * jnp.bitwise_and(where[1] + za, 3) + jnp.bitwise_and(where[0] + (step + 4), 3)
            for core in range(2):
                for kind in range(2):
                    lane = (4 * kind + at) * half
                    out[chip, core, :, kind * half : (kind + 1) * half] = got[
                        core * QUAD + za, :, lane : lane + half
                    ]


def combine_kernel(where, same, cross, home, to_same, to_cross):
    experts, cap, half = home.shape[0], home.shape[2], home.shape[3] // 2
    for packed, side, out in (
        (same, where[0], to_same),
        (cross, 1 - where[0], to_cross),
    ):
        rows = out.shape[0]
        chosen, weights = selection(packed, experts * cap)
        columns = jnp.concatenate(weights * 4, axis=0).T
        slots = jnp.concatenate(
            [home[expert, side].astype(F32) for expert in range(experts)], axis=0
        ).astype(BF)
        one, two = chosen[0].astype(BF), chosen[1].astype(BF)
        out[:, :half] = (
            columns[:, 0:1] * contract(one, slots[:, :half], 0, 0)
            + columns[:, 1:2] * contract(two, slots[:, :half], 0, 0)
        ).astype(BF)
        out[:, half:] = contract(one + two, slots[:, half:], 0, 0).astype(BF)


def unpack_kernel(where, same, cross, mixed, grad):
    half = same.shape[1] // 2
    first = where[0] == 0
    for kind, out in enumerate((mixed, grad)):
        lanes = slice(kind * half, (kind + 1) * half)
        out[:, :half] = jnp.where(first, same[:, lanes], cross[:, lanes])
        out[:, half:] = jnp.where(first, cross[:, lanes], same[:, lanes])


def partial_sum(slots, weights, side, rows, part):
    width, half = weights[0].shape[1] // 3, weights[0].shape[0]
    start = pl.multiple_of(side * rows, rows)
    total = None
    for at, w in enumerate(weights):
        lane = (4 * (part // 2) + at) * half
        term = contract(
            slots[pl.ds(start, rows), lane : lane + half],
            w[:, part * width : (part + 1) * width],
            1,
            0,
        )
        total = term if total is None else total + term
    return total


def sibling_kernel(where, slots, w0, w1, w2, w3, out):
    quads, cap, width = out.shape[0], out.shape[1], w0.shape[1] // 3
    for part in range(3):
        total = partial_sum(slots, (w0, w1, w2, w3), 1 - where[0], quads * cap, part)
        for quad in range(quads):
            out[quad, :, part * width : (part + 1) * width] = total[
                quad * cap : (quad + 1) * cap
            ].astype(out.dtype)


def split_kernel(
    where, slots, w0, w1, w2, w3, other, far_right, far_left, own, ahead, behind, mine
):
    quads, cap, width = other.shape[0], other.shape[1], w0.shape[1] // 3
    core, me, cut = where[0], where[1], far_right.shape[1]
    for part in range(3):
        lanes = slice(part * width, (part + 1) * width)
        total = partial_sum(slots, (w0, w1, w2, w3), core, quads * cap, part)
        for quad in range(quads):
            mine[quad, :, lanes] = total[quad * cap : (quad + 1) * cap] + other[
                quad, :, lanes
            ].astype(F32)

    def piece(step, lanes):
        return mine[jnp.bitwise_and(me + step, QUAD - 1), :, lanes]

    whole = slice(0, 2 * cut)
    far_right[...] = piece(2, slice(0, cut)).astype(BF)
    far_left[...] = piece(2, slice(cut, 2 * cut)).astype(BF)
    own[...] = piece(0, whole)
    ahead[...] = piece(1, whole)
    behind[...] = piece(3, whole)


def relay_kernel(ahead, behind, from_left, from_right, to_right, to_left):
    cut = from_left.shape[1]
    to_right[:, :cut] = (ahead[:, :cut] + from_left[...].astype(F32)).astype(BF)
    to_right[:, cut:] = ahead[:, cut:].astype(BF)
    to_left[:, :cut] = behind[:, :cut].astype(BF)
    to_left[:, cut:] = (behind[:, cut:] + from_right[...].astype(F32)).astype(BF)


def activate_kernel(own, from_left, from_right, out):
    width = own.shape[1] // 3

    def total(start):
        lanes = slice(start, start + width)
        return own[:, lanes] + from_left[:, lanes].astype(F32) + from_right[:, lanes].astype(F32)

    gate_val, up_val, back_hidden = total(0), total(width), total(2 * width)
    sigmoid_gate = jax.nn.sigmoid(gate_val)
    active = gate_val * sigmoid_gate
    out[:, :width] = (
        back_hidden * up_val * sigmoid_gate * (1.0 + gate_val * (1.0 - sigmoid_gate))
    ).astype(BF)
    out[:, width : 2 * width] = (back_hidden * active).astype(BF)
    out[:, 2 * width :] = (active * up_val).astype(BF)


def outs_kernel(rows, w0, w1, w2, w3, out):
    width, half = w0.shape[1] // 3, w0.shape[0]
    for at, w in enumerate((w0, w1, w2, w3)):
        value = contract(rows[:, 2 * width :], w[:, 2 * width :], 1, 1)
        out[:, at * half : (at + 1) * half] = value.astype(BF)
        value = contract(rows[:, : 2 * width], w[:, : 2 * width], 1, 1)
        out[:, (4 + at) * half : (5 + at) * half] = value.astype(BF)


def grads_kernel(slots, rows, g0, g1, g2, g3):
    width, half = g0.shape[1] // 3, g0.shape[0]
    for at, g in enumerate((g0, g1, g2, g3)):
        left = slots[:, at * half : (at + 1) * half]
        value = contract(left, rows[:, : 2 * width], 0, 0)
        g[:, : 2 * width] = value.astype(g.dtype)
        left = slots[:, (4 + at) * half : (5 + at) * half]
        value = contract(left, rows[:, 2 * width :], 0, 0)
        g[:, 2 * width :] = value.astype(g.dtype)


def finish_kernel(g0, g1, g2, g3, ng, nu, nd, mg, sg, mu, su, md, sd):
    width = ng.shape[2]

    def total(start):
        lanes = slice(start, start + width)
        return (g0[:, lanes] + g1[:, lanes].astype(F32)) + (
            g2[:, lanes].astype(F32) + g3[:, lanes].astype(F32)
        )

    gate = total(0)
    mg[0] = gate
    sg[0] = gate * ng[0].astype(F32)
    up = total(width)
    mu[0] = up
    su[0] = up * nu[0].astype(F32)
    down = total(2 * width).T
    md[0] = down
    sd[0] = down * nd[0].astype(F32)


def ones_where(condition):
    return jnp.where(condition, 1.0, 0.0).astype(F32)


def place_routes(route, experts):
    rows = route.shape[1]
    names = lax.broadcasted_iota(jnp.int32, (experts, rows), 0)
    first = ones_where(route[0:1] == names)
    second = ones_where(route[1:2] == names)
    before = ones_where(
        lax.broadcasted_iota(jnp.int32, (rows, rows), 0)
        < lax.broadcasted_iota(jnp.int32, (rows, rows), 1)
    ).astype(BF)
    earlier = contract((first + second).astype(BF), before, 1, 0)
    return [
        route[0:1].astype(F32),
        route[1:2].astype(F32),
        jnp.sum(earlier * first, axis=0, keepdims=True),
        jnp.sum((earlier + first) * second, axis=0, keepdims=True),
    ]


def body(
    tokens,
    cotangent,
    route,
    route_weight,
    mean_gate,
    spread_gate,
    noise_gate,
    mean_up,
    spread_up,
    noise_up,
    mean_down,
    spread_down,
    noise_down,
):
    experts = lax.axis_size(PLANE)
    group_rows, routes = route.shape
    feats = tokens.shape[1]
    half = feats // 2
    width = mean_gate.shape[2]
    cap = group_rows * routes // experts * 3 // 2
    rows_all = 2 * QUAD * cap
    me = lax.axis_index("za").astype(jnp.int32).reshape(1)
    zb = lax.axis_index("zb").astype(jnp.int32).reshape(1)
    core = lax.axis_index("core").astype(jnp.int32).reshape(1)

    routed = (route.T, route_weight.T, tokens, cotangent)
    packed = pl.pallas_call(
        pack_kernel,
        out_shape=(jax.ShapeDtypeStruct((group_rows + NOTES, 2 * half), BF),) * 2,
        in_specs=[pl.BlockSpec(memory_space=pltpu.SMEM)]
        + [pl.BlockSpec(memory_space=pltpu.HBM)] * 4,
        out_specs=(pl.BlockSpec(memory_space=pltpu.VMEM),) * 2,
        scratch_shapes=[pltpu.VMEM(a.shape, a.dtype) for a in routed]
        + [pltpu.SemaphoreType.DMA((4,))],
        compiler_params=pltpu.CompilerParams(vmem_limit_bytes=60 * 1024 * 1024),
    )(core, *routed)
    same = to_window(packed[0], False)
    cross = to_window(packed[1], True)
    w_own = pl.pallas_call(
        sample_kernel,
        out_shape=jax.ShapeDtypeStruct((half, 3 * width), BF),
        in_specs=[pl.BlockSpec(memory_space=pltpu.HBM)] * 9,
        out_specs=pl.BlockSpec(memory_space=pltpu.VMEM),
        scratch_shapes=[
            pltpu.VMEM((6, half, width), BF),
            pltpu.VMEM((3, width, half), BF),
            pltpu.SemaphoreType.DMA((9,)),
        ],
        compiler_params=pltpu.CompilerParams(vmem_limit_bytes=60 * 1024 * 1024),
    )(
        mean_gate,
        spread_gate,
        noise_gate,
        mean_up,
        spread_up,
        noise_up,
        mean_down,
        spread_down,
        noise_down,
    )
    w_own, same, cross = lax.optimization_barrier((w_own, same, cross))
    weights = (
        w_own,
        along_ring(w_own, (-1, -1)),
        along_ring(w_own, (1, 1)),
        along_ring(w_own, (-2, 2)),
    )

    (send,) = kernel_call(
        pick_kernel,
        [jax.ShapeDtypeStruct((experts, 2, cap, 2 * half), BF)],
        core,
        same,
        cross,
        scalars=1,
    )
    got = lax.all_to_all(send, PLANE, split_axis=0, concat_axis=0, tiled=True)
    (got,) = kernel_call(
        spread_kernel,
        [jax.ShapeDtypeStruct((2 * QUAD, cap, 8 * half), BF)],
        jnp.concatenate([zb, me]),
        got,
        scalars=1,
    )
    slots = got.reshape(rows_all, 8 * half)

    (other,) = kernel_call(
        sibling_kernel,
        [jax.ShapeDtypeStruct((QUAD, cap, 3 * width), BF)],
        core,
        slots,
        *weights,
        scalars=1,
    )
    other = lax.ppermute(other, "core", [(0, 1), (1, 0)])
    cut = 3 * width // 2
    total = jax.ShapeDtypeStruct((cap, 3 * width), F32)
    wire = jax.ShapeDtypeStruct((cap, 3 * width), BF)
    half_wire = jax.ShapeDtypeStruct((cap, cut), BF)
    far_right, far_left, own, ahead, behind = kernel_call(
        split_kernel,
        [half_wire] * 2 + [total] * 3,
        jnp.concatenate([core, me]),
        slots,
        *weights,
        other,
        scalars=1,
        scratch=[pltpu.VMEM((QUAD, cap, 3 * width), F32)],
    )
    to_right, to_left = kernel_call(
        relay_kernel, [wire] * 2, ahead, behind, shift(far_right, 1), shift(far_left, -1)
    )
    (rows,) = kernel_call(
        activate_kernel, [wire], own, shift(to_right, 1), shift(to_left, -1)
    )

    rows = lax.all_gather(rows, "za", axis=0, tiled=True)
    rows = lax.all_gather(rows, "core", axis=0, tiled=True)
    (outs,) = kernel_call(
        outs_kernel, [jax.ShapeDtypeStruct((rows_all, 8 * half), BF)], rows, *weights
    )
    outs = outs.reshape(2 * QUAD, cap, 8 * half)
    w_sent = kernel_call(
        grads_kernel,
        [jax.ShapeDtypeStruct((half, 3 * width), F32)]
        + [jax.ShapeDtypeStruct((half, 3 * width), BF)] * 3,
        slots,
        rows,
    )
    w_grads = (
        w_sent[0],
        along_ring(w_sent[1], (1, 1)),
        along_ring(w_sent[2], (-1, -1)),
        along_ring(w_sent[3], (2, -2)),
    )

    (home,) = kernel_call(
        collect_kernel,
        [jax.ShapeDtypeStruct((experts, 2, cap, 2 * half), BF)],
        jnp.concatenate([zb, me]),
        outs,
        w_sent[3],
        scalars=1,
        free=1,
    )
    home = lax.all_to_all(home, PLANE, split_axis=0, concat_axis=0, tiled=True)
    ready = kernel_call(
        combine_kernel,
        [jax.ShapeDtypeStruct((group_rows, 2 * half), BF)] * 2,
        core,
        same,
        cross,
        home,
        scalars=1,
    )
    mixed_out, token_grad = kernel_call(
        unpack_kernel,
        [jax.ShapeDtypeStruct((group_rows, feats), BF)] * 2,
        core,
        to_window(ready[0], False, True),
        to_window(ready[1], True, True),
        scalars=1,
    )
    by_row = jax.ShapeDtypeStruct((1, half, width), F32)
    by_column = jax.ShapeDtypeStruct((1, width, half), F32)
    ends = kernel_call(
        finish_kernel,
        [by_row] * 4 + [by_column] * 2,
        *w_grads,
        noise_gate,
        noise_up,
        noise_down,
    )
    return (mixed_out, token_grad) + tuple(ends)


def solution(mesh):
    fine = Mesh(mesh.devices.reshape(4, 4, QUAD, 4, 2), PLANE + RING)
    by_token = P(RING, PLANE)
    by_group = P(RING, None)
    by_row = P(PLANE, RING, None)
    by_column = P(PLANE, None, RING)
    return jax.shard_map(
        body,
        mesh=fine,
        in_specs=(by_token,) * 2 + (by_group,) * 2 + (by_row,) * 6 + (by_column,) * 3,
        out_specs=(by_token,) * 2 + (by_row,) * 4 + (by_column,) * 2,
        check_vma=False,
    )
```

```python
import itertools

import jax
import jax.numpy as jnp
from jax import lax
from jax.experimental import pallas as pl
from jax.experimental.pallas import tpu as pltpu
from jax.sharding import Mesh, PartitionSpec as P

BF = jnp.bfloat16
F32 = jnp.float32
PLANE = ("y", "x")
RING = ("za", "zb", "core")
QUAD = 4
NOTES = 16
WINDOW = ((0, 1, -1, 2), (0, 1, -1, -2))


def sampled(mean_part, spread, noise_part):
    return (mean_part.astype(F32) + spread.astype(F32) * noise_part.astype(F32)).astype(BF)


def contract(left_side, right_side, left_dim, right_dim):
    return lax.dot_general(
        left_side,
        right_side,
        (((left_dim,), (right_dim,)), ((), ())),
        preferred_element_type=F32,
    )


def shift(value, step):
    return lax.ppermute(value, "za", [(i, (i + step) % QUAD) for i in range(QUAD)])


def along_ring(value, steps):
    chips = lax.axis_size("za") * lax.axis_size("zb")
    pairs = [
        (2 * z + core, 2 * ((z + steps[core]) % chips) + core)
        for z in range(chips)
        for core in range(2)
    ]
    return lax.ppermute(value, RING, pairs)


def to_window(value, cross, back=False):
    sizes = [lax.axis_size(name) for name in PLANE + RING]
    quads = sizes[3]

    def index(place):
        number = 0
        for size, at in zip(sizes, place):
            number = number * size + at
        return number

    pairs = []
    for y, x, za, zb, core in itertools.product(*map(range, sizes)):
        side = 1 - core if cross else core
        near = (zb + quads // 2) % quads
        for goal in range(QUAD):
            for step in WINDOW[side]:
                if (quads * goal + near + step - quads * y - x) % (QUAD * quads) == 0:
                    pair = (
                        index((y, x, za, zb, core)),
                        index(((za + goal) % QUAD, x, goal, near, side)),
                    )
                    pairs.append(pair[::-1] if back else pair)
    return lax.ppermute(value, PLANE + RING, pairs)


def kernel_call(kernel, outs, *operands, free=0, scalars=0, scratch=()):
    whole = pl.BlockSpec(memory_space=pltpu.VMEM)
    count = len(operands) - free - scalars
    moved = sum(a.size * a.dtype.itemsize for a in operands) + sum(
        o.size * o.dtype.itemsize for o in outs
    )
    return pl.pallas_call(
        kernel,
        out_shape=tuple(outs),
        in_specs=[pl.BlockSpec(memory_space=pltpu.SMEM)] * scalars
        + [whole] * count
        + [pl.BlockSpec(memory_space=pl.ANY)] * free,
        out_specs=(whole,) * len(outs),
        scratch_shapes=list(scratch),
        compiler_params=pltpu.CompilerParams(vmem_limit_bytes=8 * 1024 * 1024),
        cost_estimate=pl.CostEstimate(flops=0, bytes_accessed=moved, transcendentals=0),
    )(*operands)


def sample_kernel(*refs):
    sources, (out, rows, columns, done) = refs[:9], refs[-4:]
    places = [rows.at[i] for i in range(6)] + [columns.at[i] for i in range(3)]
    copies = [
        pltpu.make_async_copy(source.at[0], place, done.at[i])
        for i, (source, place) in enumerate(zip(sources, places))
    ]
    for copy in copies:
        copy.start()
    width = rows.shape[2]
    for part in range(2):
        for copy in copies[3 * part : 3 * part + 3]:
            copy.wait()
        out[:, part * width : (part + 1) * width] = sampled(
            rows[3 * part], rows[3 * part + 1], rows[3 * part + 2]
        )
    for copy in copies[6:]:
        copy.wait()
    down = columns[0].astype(F32) + columns[1].astype(F32) * columns[2].astype(F32)
    out[:, 2 * width :] = down.T.astype(BF)


def pack_kernel(where, *refs):
    sources, (same, cross), places, done = refs[:4], refs[4:6], refs[6:10], refs[10]
    copies = [
        pltpu.make_async_copy(source, place, done.at[i])
        for i, (source, place) in enumerate(zip(sources, places))
    ]
    for copy in copies:
        copy.start()
    for copy in copies:
        copy.wait()
    route, weight, tokens, cotangent = places
    rows, half = tokens.shape[0], tokens.shape[1] // 2
    notes = place_routes(route[...], 4 * QUAD)
    for r in range(2):
        rest = weight[r : r + 1]
        for _ in range(3):
            term = rest.astype(BF).astype(F32)
            notes.append(term)
            rest = rest - term
    notes.append(jnp.zeros((NOTES - len(notes), rows), F32))
    table = jnp.concatenate(notes, axis=0).astype(BF)
    core = where[0]
    for out, side in ((same, core), (cross, 1 - core)):
        for kind, source in enumerate((tokens, cotangent)):
            lanes = slice(kind * half, (kind + 1) * half)
            out[:rows, lanes] = jnp.where(side == 0, source[:, :half], source[:, half:])
            out[rows:, lanes] = table[:, :half]


def selection(packed, slots):
    rows = packed.shape[0] - NOTES
    notes = packed[rows:, :rows].astype(F32)
    names = lax.broadcasted_iota(jnp.int32, (slots, rows), 0)
    chosen, weights = [], []
    for r in range(2):
        cap = slots // (4 * QUAD)
        target = (notes[r : r + 1] * cap + notes[2 + r : 3 + r]).astype(jnp.int32)
        chosen.append(ones_where(target == names))
        at = 4 + 3 * r
        weights.append((notes[at : at + 1] + notes[at + 1 : at + 2]) + notes[at + 2 : at + 3])
    return chosen, weights


def pick_kernel(where, same, cross, out):
    experts, cap, half = out.shape[0], out.shape[2], out.shape[3] // 2
    rows = same.shape[0] - NOTES
    for packed, side in ((same, where[0]), (cross, 1 - where[0])):
        chosen, weights = selection(packed, experts * cap)
        both = (chosen[0] + chosen[1]).astype(BF)
        weight = jnp.sum(
            chosen[0] * weights[0] + chosen[1] * weights[1], axis=1, keepdims=True
        )
        x = contract(both, packed[:rows, :half], 1, 0)
        d = weight * contract(both, packed[:rows, half:], 1, 0)
        for expert in range(experts):
            at = slice(expert * cap, (expert + 1) * cap)
            out[expert, side, :, :half] = x[at].astype(BF)
            out[expert, side, :, half:] = d[at].astype(BF)


def spread_kernel(where, got, out):
    half = got.shape[3] // 2
    for za in range(QUAD):
        for at, step in enumerate(WINDOW[0]):
            chip = 4 * jnp.bitwise_and(where[1] + za, 3) + jnp.bitwise_and(where[0] + (step + 4), 3)
            for core in range(2):
                for kind in range(2):
                    lane = (4 * kind + at) * half
                    out[core * QUAD + za, :, lane : lane + half] = got[
                        chip, core, :, kind * half : (kind + 1) * half
                    ]


def collect_kernel(where, got, *rest):
    out = rest[-1]
    half = out.shape[3] // 2
    for za in range(QUAD):
        for at, step in enumerate(WINDOW[0]):
            chip = 4 * jnp.bitwise_and(where[1] + za, 3) + jnp.bitwise_and(where[0] + (step + 4), 3)
            for core in range(2):
                for kind in range(2):
                    lane = (4 * kind + at) * half
                    out[chip, core, :, kind * half : (kind + 1) * half] = got[
                        core * QUAD + za, :, lane : lane + half
                    ]


def combine_kernel(where, same, cross, home, to_same, to_cross):
    experts, cap, half = home.shape[0], home.shape[2], home.shape[3] // 2
    for packed, side, out in (
        (same, where[0], to_same),
        (cross, 1 - where[0], to_cross),
    ):
        rows = out.shape[0]
        chosen, weights = selection(packed, experts * cap)
        columns = jnp.concatenate(weights * 4, axis=0).T
        slots = jnp.concatenate(
            [home[expert, side].astype(F32) for expert in range(experts)], axis=0
        ).astype(BF)
        one, two = chosen[0].astype(BF), chosen[1].astype(BF)
        out[:, :half] = (
            columns[:, 0:1] * contract(one, slots[:, :half], 0, 0)
            + columns[:, 1:2] * contract(two, slots[:, :half], 0, 0)
        ).astype(BF)
        out[:, half:] = contract(one + two, slots[:, half:], 0, 0).astype(BF)


def unpack_kernel(where, same, cross, after, mixed, grad):
    del after
    half = same.shape[1] // 2
    first = where[0] == 0
    for kind, out in enumerate((mixed, grad)):
        lanes = slice(kind * half, (kind + 1) * half)
        out[:, :half] = jnp.where(first, same[:, lanes], cross[:, lanes])
        out[:, half:] = jnp.where(first, cross[:, lanes], same[:, lanes])


def partial_sum(slots, weights, side, rows, part):
    width, half = weights[0].shape[1] // 3, weights[0].shape[0]
    start = pl.multiple_of(side * rows, rows)
    total = None
    for at, w in enumerate(weights):
        lane = (4 * (part // 2) + at) * half
        term = contract(
            slots[pl.ds(start, rows), lane : lane + half],
            w[:, part * width : (part + 1) * width],
            1,
            0,
        )
        total = term if total is None else total + term
    return total


def sibling_kernel(where, slots, w0, w1, w2, w3, out):
    quads, cap, width = out.shape[0], out.shape[1], w0.shape[1] // 3
    for part in range(3):
        total = partial_sum(slots, (w0, w1, w2, w3), 1 - where[0], quads * cap, part)
        for quad in range(quads):
            out[quad, :, part * width : (part + 1) * width] = total[
                quad * cap : (quad + 1) * cap
            ].astype(out.dtype)


def split_kernel(
    where, slots, w0, w1, w2, w3, other, far_right, far_left, own, ahead, behind, mine
):
    quads, cap, width = other.shape[0], other.shape[1], w0.shape[1] // 3
    core, me, cut = where[0], where[1], far_right.shape[1]
    for part in range(3):
        lanes = slice(part * width, (part + 1) * width)
        total = partial_sum(slots, (w0, w1, w2, w3), core, quads * cap, part)
        for quad in range(quads):
            mine[quad, :, lanes] = total[quad * cap : (quad + 1) * cap] + other[
                quad, :, lanes
            ].astype(F32)

    def piece(step, lanes):
        return mine[jnp.bitwise_and(me + step, QUAD - 1), :, lanes]

    whole = slice(0, 2 * cut)
    far_right[...] = piece(2, slice(0, cut)).astype(BF)
    far_left[...] = piece(2, slice(cut, 2 * cut)).astype(BF)
    own[...] = piece(0, whole)
    ahead[...] = piece(1, whole)
    behind[...] = piece(3, whole)


def relay_kernel(ahead, behind, from_left, from_right, to_right, to_left):
    cut = from_left.shape[1]
    to_right[:, :cut] = (ahead[:, :cut] + from_left[...].astype(F32)).astype(BF)
    to_right[:, cut:] = ahead[:, cut:].astype(BF)
    to_left[:, :cut] = behind[:, :cut].astype(BF)
    to_left[:, cut:] = (behind[:, cut:] + from_right[...].astype(F32)).astype(BF)


def activate_kernel(own, from_left, from_right, out):
    width = own.shape[1] // 3

    def total(start):
        lanes = slice(start, start + width)
        return own[:, lanes] + from_left[:, lanes].astype(F32) + from_right[:, lanes].astype(F32)

    gate_val, up_val, back_hidden = total(0), total(width), total(2 * width)
    sigmoid_gate = jax.nn.sigmoid(gate_val)
    active = gate_val * sigmoid_gate
    out[:, :width] = (
        back_hidden * up_val * sigmoid_gate * (1.0 + gate_val * (1.0 - sigmoid_gate))
    ).astype(BF)
    out[:, width : 2 * width] = (back_hidden * active).astype(BF)
    out[:, 2 * width :] = (active * up_val).astype(BF)


def outs_kernel(rows, w0, w1, w2, w3, out):
    width, half = w0.shape[1] // 3, w0.shape[0]
    for at, w in enumerate((w0, w1, w2, w3)):
        value = contract(rows[:, 2 * width :], w[:, 2 * width :], 1, 1)
        out[:, at * half : (at + 1) * half] = value.astype(BF)
        value = contract(rows[:, : 2 * width], w[:, : 2 * width], 1, 1)
        out[:, (4 + at) * half : (5 + at) * half] = value.astype(BF)


def grads_kernel(slots, rows, g0, g1, g2, g3):
    width, half = g0.shape[1] // 3, g0.shape[0]
    for at, g in enumerate((g0, g1, g2, g3)):
        left = slots[:, at * half : (at + 1) * half]
        value = contract(left, rows[:, : 2 * width], 0, 0)
        g[:, : 2 * width] = value.astype(g.dtype)
        left = slots[:, (4 + at) * half : (5 + at) * half]
        value = contract(left, rows[:, 2 * width :], 0, 0)
        g[:, 2 * width :] = value.astype(g.dtype)


def finish_kernel(g0, g1, g2, g3, ng, nu, nd, mg, sg, mu, su, md, sd, done):
    width = ng.shape[2]

    def total(start):
        lanes = slice(start, start + width)
        return (g0[:, lanes] + g1[:, lanes].astype(F32)) + (
            g2[:, lanes].astype(F32) + g3[:, lanes].astype(F32)
        )

    gate = total(0)
    mg[0] = gate
    sg[0] = gate * ng[0].astype(F32)
    up = total(width)
    mu[0] = up
    su[0] = up * nu[0].astype(F32)
    down = total(2 * width).T
    md[0] = down
    sd[0] = down * nd[0].astype(F32)
    done[...] = jnp.zeros_like(done)


def ones_where(condition):
    return jnp.where(condition, 1.0, 0.0).astype(F32)


def place_routes(route, experts):
    rows = route.shape[1]
    names = lax.broadcasted_iota(jnp.int32, (experts, rows), 0)
    first = ones_where(route[0:1] == names)
    second = ones_where(route[1:2] == names)
    before = ones_where(
        lax.broadcasted_iota(jnp.int32, (rows, rows), 0)
        < lax.broadcasted_iota(jnp.int32, (rows, rows), 1)
    ).astype(BF)
    earlier = contract((first + second).astype(BF), before, 1, 0)
    return [
        route[0:1].astype(F32),
        route[1:2].astype(F32),
        jnp.sum(earlier * first, axis=0, keepdims=True),
        jnp.sum((earlier + first) * second, axis=0, keepdims=True),
    ]


def body(
    tokens,
    cotangent,
    route,
    route_weight,
    mean_gate,
    spread_gate,
    noise_gate,
    mean_up,
    spread_up,
    noise_up,
    mean_down,
    spread_down,
    noise_down,
):
    experts = lax.axis_size(PLANE)
    group_rows, routes = route.shape
    feats = tokens.shape[1]
    half = feats // 2
    width = mean_gate.shape[2]
    cap = group_rows * routes // experts * 3 // 2
    rows_all = 2 * QUAD * cap
    me = lax.axis_index("za").astype(jnp.int32).reshape(1)
    zb = lax.axis_index("zb").astype(jnp.int32).reshape(1)
    core = lax.axis_index("core").astype(jnp.int32).reshape(1)

    routed = (route.T, route_weight.T, tokens, cotangent)
    packed = pl.pallas_call(
        pack_kernel,
        out_shape=(jax.ShapeDtypeStruct((group_rows + NOTES, 2 * half), BF),) * 2,
        in_specs=[pl.BlockSpec(memory_space=pltpu.SMEM)]
        + [pl.BlockSpec(memory_space=pltpu.HBM)] * 4,
        out_specs=(pl.BlockSpec(memory_space=pltpu.VMEM),) * 2,
        scratch_shapes=[pltpu.VMEM(a.shape, a.dtype) for a in routed]
        + [pltpu.SemaphoreType.DMA((4,))],
        compiler_params=pltpu.CompilerParams(vmem_limit_bytes=60 * 1024 * 1024),
    )(core, *routed)
    same = to_window(packed[0], False)
    cross = to_window(packed[1], True)
    w_own = pl.pallas_call(
        sample_kernel,
        out_shape=jax.ShapeDtypeStruct((half, 3 * width), BF),
        in_specs=[pl.BlockSpec(memory_space=pltpu.HBM)] * 9,
        out_specs=pl.BlockSpec(memory_space=pltpu.VMEM),
        scratch_shapes=[
            pltpu.VMEM((6, half, width), BF),
            pltpu.VMEM((3, width, half), BF),
            pltpu.SemaphoreType.DMA((9,)),
        ],
        compiler_params=pltpu.CompilerParams(vmem_limit_bytes=60 * 1024 * 1024),
    )(
        mean_gate,
        spread_gate,
        noise_gate,
        mean_up,
        spread_up,
        noise_up,
        mean_down,
        spread_down,
        noise_down,
    )
    w_own, same, cross = lax.optimization_barrier((w_own, same, cross))
    weights = (
        w_own,
        along_ring(w_own, (-1, -1)),
        along_ring(w_own, (1, 1)),
        along_ring(w_own, (-2, 2)),
    )

    (send,) = kernel_call(
        pick_kernel,
        [jax.ShapeDtypeStruct((experts, 2, cap, 2 * half), BF)],
        core,
        same,
        cross,
        scalars=1,
    )
    got = lax.all_to_all(send, PLANE, split_axis=0, concat_axis=0, tiled=True)
    (got,) = kernel_call(
        spread_kernel,
        [jax.ShapeDtypeStruct((2 * QUAD, cap, 8 * half), BF)],
        jnp.concatenate([zb, me]),
        got,
        scalars=1,
    )
    slots = got.reshape(rows_all, 8 * half)

    (other,) = kernel_call(
        sibling_kernel,
        [jax.ShapeDtypeStruct((QUAD, cap, 3 * width), BF)],
        core,
        slots,
        *weights,
        scalars=1,
    )
    other = lax.ppermute(other, "core", [(0, 1), (1, 0)])
    cut = 3 * width // 2
    total = jax.ShapeDtypeStruct((cap, 3 * width), F32)
    wire = jax.ShapeDtypeStruct((cap, 3 * width), BF)
    half_wire = jax.ShapeDtypeStruct((cap, cut), BF)
    far_right, far_left, own, ahead, behind = kernel_call(
        split_kernel,
        [half_wire] * 2 + [total] * 3,
        jnp.concatenate([core, me]),
        slots,
        *weights,
        other,
        scalars=1,
        scratch=[pltpu.VMEM((QUAD, cap, 3 * width), F32)],
    )
    to_right, to_left = kernel_call(
        relay_kernel, [wire] * 2, ahead, behind, shift(far_right, 1), shift(far_left, -1)
    )
    (rows,) = kernel_call(
        activate_kernel, [wire], own, shift(to_right, 1), shift(to_left, -1)
    )

    rows = lax.all_gather(rows, "za", axis=0, tiled=True)
    rows = lax.all_gather(rows, "core", axis=0, tiled=True)
    (outs,) = kernel_call(
        outs_kernel, [jax.ShapeDtypeStruct((rows_all, 8 * half), BF)], rows, *weights
    )
    outs = outs.reshape(2 * QUAD, cap, 8 * half)
    w_sent = kernel_call(
        grads_kernel,
        [jax.ShapeDtypeStruct((half, 3 * width), F32)]
        + [jax.ShapeDtypeStruct((half, 3 * width), BF)] * 3,
        slots,
        rows,
    )
    w_grads = (
        w_sent[0],
        along_ring(w_sent[1], (1, 1)),
        along_ring(w_sent[2], (-1, -1)),
        along_ring(w_sent[3], (2, -2)),
    )

    (home,) = kernel_call(
        collect_kernel,
        [jax.ShapeDtypeStruct((experts, 2, cap, 2 * half), BF)],
        jnp.concatenate([zb, me]),
        outs,
        w_sent[3],
        scalars=1,
        free=1,
    )
    home = lax.all_to_all(home, PLANE, split_axis=0, concat_axis=0, tiled=True)
    ready = kernel_call(
        combine_kernel,
        [jax.ShapeDtypeStruct((group_rows, 2 * half), BF)] * 2,
        core,
        same,
        cross,
        home,
        scalars=1,
    )
    by_row = jax.ShapeDtypeStruct((1, half, width), F32)
    by_column = jax.ShapeDtypeStruct((1, width, half), F32)
    ends = kernel_call(
        finish_kernel,
        [by_row] * 4 + [by_column] * 2 + [jax.ShapeDtypeStruct((8, 128), F32)],
        *w_grads,
        noise_gate,
        noise_up,
        noise_down,
    )
    mixed_out, token_grad = kernel_call(
        unpack_kernel,
        [jax.ShapeDtypeStruct((group_rows, feats), BF)] * 2,
        core,
        to_window(ready[0], False, True),
        to_window(ready[1], True, True),
        ends[6],
        scalars=1,
        free=1,
    )
    return (mixed_out, token_grad) + tuple(ends[:6])


def solution(mesh):
    fine = Mesh(mesh.devices.reshape(4, 4, QUAD, 4, 2), PLANE + RING)
    by_token = P(RING, PLANE)
    by_group = P(RING, None)
    by_row = P(PLANE, RING, None)
    by_column = P(PLANE, None, RING)
    return jax.shard_map(
        body,
        mesh=fine,
        in_specs=(by_token,) * 2 + (by_group,) * 2 + (by_row,) * 6 + (by_column,) * 3,
        out_specs=(by_token,) * 2 + (by_row,) * 4 + (by_column,) * 2,
        check_vma=False,
    )
```

```python
import itertools

import jax
import jax.numpy as jnp
from jax import lax
from jax.experimental import pallas as pl
from jax.experimental.pallas import tpu as pltpu
from jax.sharding import Mesh, PartitionSpec as P

BF = jnp.bfloat16
F32 = jnp.float32
PLANE = ("y", "x")
RING = ("za", "zb", "core")
QUAD = 4
NOTES = 16
WINDOW = ((0, 1, -1, 2), (0, 1, -1, -2))


def sampled(mean_part, spread, noise_part):
    return (mean_part.astype(F32) + spread.astype(F32) * noise_part.astype(F32)).astype(BF)


def contract(left_side, right_side, left_dim, right_dim):
    return lax.dot_general(
        left_side,
        right_side,
        (((left_dim,), (right_dim,)), ((), ())),
        preferred_element_type=F32,
    )


def shift(value, step):
    return lax.ppermute(value, "za", [(i, (i + step) % QUAD) for i in range(QUAD)])


def along_ring(value, steps):
    chips = lax.axis_size("za") * lax.axis_size("zb")
    pairs = [
        (2 * z + core, 2 * ((z + steps[core]) % chips) + core)
        for z in range(chips)
        for core in range(2)
    ]
    return lax.ppermute(value, RING, pairs)


def to_window(value, cross, back=False):
    sizes = [lax.axis_size(name) for name in PLANE + RING]
    quads = sizes[3]

    def index(place):
        number = 0
        for size, at in zip(sizes, place):
            number = number * size + at
        return number

    pairs = []
    for y, x, za, zb, core in itertools.product(*map(range, sizes)):
        side = 1 - core if cross else core
        near = (zb + quads // 2) % quads
        for goal in range(QUAD):
            for step in WINDOW[side]:
                if (quads * goal + near + step - quads * y - x) % (QUAD * quads) == 0:
                    pair = (
                        index((y, x, za, zb, core)),
                        index(((za + goal) % QUAD, x, goal, near, side)),
                    )
                    pairs.append(pair[::-1] if back else pair)
    return lax.ppermute(value, PLANE + RING, pairs)


def kernel_call(kernel, outs, *operands, free=0, scalars=0, scratch=()):
    whole = pl.BlockSpec(memory_space=pltpu.VMEM)
    count = len(operands) - free - scalars
    moved = sum(a.size * a.dtype.itemsize for a in operands) + sum(
        o.size * o.dtype.itemsize for o in outs
    )
    return pl.pallas_call(
        kernel,
        out_shape=tuple(outs),
        in_specs=[pl.BlockSpec(memory_space=pltpu.SMEM)] * scalars
        + [whole] * count
        + [pl.BlockSpec(memory_space=pl.ANY)] * free,
        out_specs=(whole,) * len(outs),
        scratch_shapes=list(scratch),
        compiler_params=pltpu.CompilerParams(vmem_limit_bytes=8 * 1024 * 1024),
        cost_estimate=pl.CostEstimate(flops=0, bytes_accessed=moved, transcendentals=0),
    )(*operands)


def sample_kernel(*refs):
    sources, (out, rows, columns, done) = refs[:9], refs[-4:]
    places = [rows.at[i] for i in range(6)] + [columns.at[i] for i in range(3)]
    copies = [
        pltpu.make_async_copy(source.at[0], place, done.at[i])
        for i, (source, place) in enumerate(zip(sources, places))
    ]
    for copy in copies:
        copy.start()
    width = rows.shape[2]
    for part in range(2):
        for copy in copies[3 * part : 3 * part + 3]:
            copy.wait()
        out[:, part * width : (part + 1) * width] = sampled(
            rows[3 * part], rows[3 * part + 1], rows[3 * part + 2]
        )
    for copy in copies[6:]:
        copy.wait()
    down = columns[0].astype(F32) + columns[1].astype(F32) * columns[2].astype(F32)
    out[:, 2 * width :] = down.T.astype(BF)


def pack_kernel(where, *refs):
    sources, (same, cross), places, done = refs[:4], refs[4:6], refs[6:10], refs[10]
    copies = [
        pltpu.make_async_copy(source, place, done.at[i])
        for i, (source, place) in enumerate(zip(sources, places))
    ]
    for copy in copies:
        copy.start()
    for copy in copies:
        copy.wait()
    route, weight, tokens, cotangent = places
    rows, half = tokens.shape[0], tokens.shape[1] // 2
    notes = place_routes(route[...], 4 * QUAD)
    for r in range(2):
        rest = weight[r : r + 1]
        for _ in range(3):
            term = rest.astype(BF).astype(F32)
            notes.append(term)
            rest = rest - term
    notes.append(jnp.zeros((NOTES - len(notes), rows), F32))
    table = jnp.concatenate(notes, axis=0).astype(BF)
    core = where[0]
    for out, side in ((same, core), (cross, 1 - core)):
        for kind, source in enumerate((tokens, cotangent)):
            lanes = slice(kind * half, (kind + 1) * half)
            out[:rows, lanes] = jnp.where(side == 0, source[:, :half], source[:, half:])
            out[rows:, lanes] = table[:, :half]


def selection(packed, slots):
    rows = packed.shape[0] - NOTES
    notes = packed[rows:, :rows].astype(F32)
    names = lax.broadcasted_iota(jnp.int32, (slots, rows), 0)
    chosen, weights = [], []
    for r in range(2):
        cap = slots // (4 * QUAD)
        target = (notes[r : r + 1] * cap + notes[2 + r : 3 + r]).astype(jnp.int32)
        chosen.append(ones_where(target == names))
        at = 4 + 3 * r
        weights.append((notes[at : at + 1] + notes[at + 1 : at + 2]) + notes[at + 2 : at + 3])
    return chosen, weights


def pick_kernel(where, same, cross, out):
    experts, cap, half = out.shape[0], out.shape[2], out.shape[3] // 2
    rows = same.shape[0] - NOTES
    for packed, side in ((same, where[0]), (cross, 1 - where[0])):
        chosen, weights = selection(packed, experts * cap)
        both = (chosen[0] + chosen[1]).astype(BF)
        weight = jnp.sum(
            chosen[0] * weights[0] + chosen[1] * weights[1], axis=1, keepdims=True
        )
        x = contract(both, packed[:rows, :half], 1, 0)
        d = weight * contract(both, packed[:rows, half:], 1, 0)
        for expert in range(experts):
            at = slice(expert * cap, (expert + 1) * cap)
            out[expert, side, :, :half] = x[at].astype(BF)
            out[expert, side, :, half:] = d[at].astype(BF)


def spread_kernel(where, got, out):
    half = got.shape[3] // 2
    for za in range(QUAD):
        for at, step in enumerate(WINDOW[0]):
            chip = 4 * jnp.bitwise_and(where[1] + za, 3) + jnp.bitwise_and(where[0] + (step + 4), 3)
            for core in range(2):
                for kind in range(2):
                    lane = (4 * kind + at) * half
                    out[core * QUAD + za, :, lane : lane + half] = got[
                        chip, core, :, kind * half : (kind + 1) * half
                    ]


def collect_kernel(where, got, *rest):
    out = rest[-1]
    half = out.shape[3] // 2
    for za in range(QUAD):
        for at, step in enumerate(WINDOW[0]):
            chip = 4 * jnp.bitwise_and(where[1] + za, 3) + jnp.bitwise_and(where[0] + (step + 4), 3)
            for core in range(2):
                for kind in range(2):
                    lane = (4 * kind + at) * half
                    out[chip, core, :, kind * half : (kind + 1) * half] = got[
                        core * QUAD + za, :, lane : lane + half
                    ]


def combine_kernel(where, same, cross, home, to_same, to_cross):
    experts, cap, half = home.shape[0], home.shape[2], home.shape[3] // 2
    for packed, side, out in (
        (same, where[0], to_same),
        (cross, 1 - where[0], to_cross),
    ):
        rows = out.shape[0]
        chosen, weights = selection(packed, experts * cap)
        columns = jnp.concatenate(weights * 4, axis=0).T
        slots = jnp.concatenate(
            [home[expert, side].astype(F32) for expert in range(experts)], axis=0
        ).astype(BF)
        one, two = chosen[0].astype(BF), chosen[1].astype(BF)
        out[:, :half] = (
            columns[:, 0:1] * contract(one, slots[:, :half], 0, 0)
            + columns[:, 1:2] * contract(two, slots[:, :half], 0, 0)
        ).astype(BF)
        out[:, half:] = contract(one + two, slots[:, half:], 0, 0).astype(BF)


def unpack_kernel(where, same, cross, after, mixed, grad):
    del after
    half = same.shape[1] // 2
    first = where[0] == 0
    for kind, out in enumerate((mixed, grad)):
        lanes = slice(kind * half, (kind + 1) * half)
        out[:, :half] = jnp.where(first, same[:, lanes], cross[:, lanes])
        out[:, half:] = jnp.where(first, cross[:, lanes], same[:, lanes])


def partial_sum(slots, weights, side, rows, part):
    width, half = weights[0].shape[1] // 3, weights[0].shape[0]
    start = pl.multiple_of(side * rows, rows)
    total = None
    for at, w in enumerate(weights):
        lane = (4 * (part // 2) + at) * half
        term = contract(
            slots[pl.ds(start, rows), lane : lane + half],
            w[:, part * width : (part + 1) * width],
            1,
            0,
        )
        total = term if total is None else total + term
    return total


def sibling_kernel(where, slots, w0, w1, w2, w3, out):
    quads, cap, width = out.shape[0], out.shape[1], w0.shape[1] // 3
    for part in range(3):
        total = partial_sum(slots, (w0, w1, w2, w3), 1 - where[0], quads * cap, part)
        for quad in range(quads):
            out[quad, :, part * width : (part + 1) * width] = total[
                quad * cap : (quad + 1) * cap
            ].astype(out.dtype)


def split_kernel(
    where, slots, w0, w1, w2, w3, other, far, behind, own, ahead, mine
):
    quads, cap, width = other.shape[0], other.shape[1], w0.shape[1] // 3
    core, me = where[0], where[1]
    for part in range(3):
        lanes = slice(part * width, (part + 1) * width)
        total = partial_sum(slots, (w0, w1, w2, w3), core, quads * cap, part)
        for quad in range(quads):
            mine[quad, :, lanes] = total[quad * cap : (quad + 1) * cap] + other[
                quad, :, lanes
            ].astype(F32)

    def piece(step):
        return mine[jnp.bitwise_and(me + step, QUAD - 1)]

    far[...] = piece(2).astype(BF)
    behind[...] = piece(3).astype(BF)
    own[...] = piece(0)
    ahead[...] = piece(1)


def relay_kernel(ahead, from_left, to_right):
    to_right[...] = (ahead[...] + from_left[...].astype(F32)).astype(BF)


def activate_kernel(own, from_left, from_right, out):
    width = own.shape[1] // 3

    def total(start):
        lanes = slice(start, start + width)
        return own[:, lanes] + from_left[:, lanes].astype(F32) + from_right[:, lanes].astype(F32)

    gate_val, up_val, back_hidden = total(0), total(width), total(2 * width)
    sigmoid_gate = jax.nn.sigmoid(gate_val)
    active = gate_val * sigmoid_gate
    out[:, :width] = (
        back_hidden * up_val * sigmoid_gate * (1.0 + gate_val * (1.0 - sigmoid_gate))
    ).astype(BF)
    out[:, width : 2 * width] = (back_hidden * active).astype(BF)
    out[:, 2 * width :] = (active * up_val).astype(BF)


def outs_kernel(rows, w0, w1, w2, w3, out):
    width, half = w0.shape[1] // 3, w0.shape[0]
    for at, w in enumerate((w0, w1, w2, w3)):
        value = contract(rows[:, 2 * width :], w[:, 2 * width :], 1, 1)
        out[:, at * half : (at + 1) * half] = value.astype(BF)
        value = contract(rows[:, : 2 * width], w[:, : 2 * width], 1, 1)
        out[:, (4 + at) * half : (5 + at) * half] = value.astype(BF)


def grads_kernel(slots, rows, g0, g1, g2, g3):
    width, half = g0.shape[1] // 3, g0.shape[0]
    for at, g in enumerate((g0, g1, g2, g3)):
        left = slots[:, at * half : (at + 1) * half]
        value = contract(left, rows[:, : 2 * width], 0, 0)
        g[:, : 2 * width] = value.astype(g.dtype)
        left = slots[:, (4 + at) * half : (5 + at) * half]
        value = contract(left, rows[:, 2 * width :], 0, 0)
        g[:, 2 * width :] = value.astype(g.dtype)


def finish_kernel(g0, g1, g2, g3, ng, nu, nd, mg, sg, mu, su, md, sd, done):
    width = ng.shape[2]

    def total(start):
        lanes = slice(start, start + width)
        return (g0[:, lanes] + g1[:, lanes].astype(F32)) + (
            g2[:, lanes].astype(F32) + g3[:, lanes].astype(F32)
        )

    gate = total(0)
    mg[0] = gate
    sg[0] = gate * ng[0].astype(F32)
    up = total(width)
    mu[0] = up
    su[0] = up * nu[0].astype(F32)
    down = total(2 * width).T
    md[0] = down
    sd[0] = down * nd[0].astype(F32)
    done[...] = jnp.zeros_like(done)


def ones_where(condition):
    return jnp.where(condition, 1.0, 0.0).astype(F32)


def place_routes(route, experts):
    rows = route.shape[1]
    names = lax.broadcasted_iota(jnp.int32, (experts, rows), 0)
    first = ones_where(route[0:1] == names)
    second = ones_where(route[1:2] == names)
    before = ones_where(
        lax.broadcasted_iota(jnp.int32, (rows, rows), 0)
        < lax.broadcasted_iota(jnp.int32, (rows, rows), 1)
    ).astype(BF)
    earlier = contract((first + second).astype(BF), before, 1, 0)
    return [
        route[0:1].astype(F32),
        route[1:2].astype(F32),
        jnp.sum(earlier * first, axis=0, keepdims=True),
        jnp.sum((earlier + first) * second, axis=0, keepdims=True),
    ]


def body(
    tokens,
    cotangent,
    route,
    route_weight,
    mean_gate,
    spread_gate,
    noise_gate,
    mean_up,
    spread_up,
    noise_up,
    mean_down,
    spread_down,
    noise_down,
):
    experts = lax.axis_size(PLANE)
    group_rows, routes = route.shape
    feats = tokens.shape[1]
    half = feats // 2
    width = mean_gate.shape[2]
    cap = group_rows * routes // experts * 3 // 2
    rows_all = 2 * QUAD * cap
    me = lax.axis_index("za").astype(jnp.int32).reshape(1)
    zb = lax.axis_index("zb").astype(jnp.int32).reshape(1)
    core = lax.axis_index("core").astype(jnp.int32).reshape(1)

    routed = (route.T, route_weight.T, tokens, cotangent)
    packed = pl.pallas_call(
        pack_kernel,
        out_shape=(jax.ShapeDtypeStruct((group_rows + NOTES, 2 * half), BF),) * 2,
        in_specs=[pl.BlockSpec(memory_space=pltpu.SMEM)]
        + [pl.BlockSpec(memory_space=pltpu.HBM)] * 4,
        out_specs=(pl.BlockSpec(memory_space=pltpu.VMEM),) * 2,
        scratch_shapes=[pltpu.VMEM(a.shape, a.dtype) for a in routed]
        + [pltpu.SemaphoreType.DMA((4,))],
        compiler_params=pltpu.CompilerParams(vmem_limit_bytes=60 * 1024 * 1024),
    )(core, *routed)
    same = to_window(packed[0], False)
    cross = to_window(packed[1], True)
    w_own = pl.pallas_call(
        sample_kernel,
        out_shape=jax.ShapeDtypeStruct((half, 3 * width), BF),
        in_specs=[pl.BlockSpec(memory_space=pltpu.HBM)] * 9,
        out_specs=pl.BlockSpec(memory_space=pltpu.VMEM),
        scratch_shapes=[
            pltpu.VMEM((6, half, width), BF),
            pltpu.VMEM((3, width, half), BF),
            pltpu.SemaphoreType.DMA((9,)),
        ],
        compiler_params=pltpu.CompilerParams(vmem_limit_bytes=60 * 1024 * 1024),
    )(
        mean_gate,
        spread_gate,
        noise_gate,
        mean_up,
        spread_up,
        noise_up,
        mean_down,
        spread_down,
        noise_down,
    )
    w_own, same, cross = lax.optimization_barrier((w_own, same, cross))
    weights = (
        w_own,
        along_ring(w_own, (-1, -1)),
        along_ring(w_own, (1, 1)),
        along_ring(w_own, (-2, 2)),
    )

    (send,) = kernel_call(
        pick_kernel,
        [jax.ShapeDtypeStruct((experts, 2, cap, 2 * half), BF)],
        core,
        same,
        cross,
        scalars=1,
    )
    got = lax.all_to_all(send, PLANE, split_axis=0, concat_axis=0, tiled=True)
    (got,) = kernel_call(
        spread_kernel,
        [jax.ShapeDtypeStruct((2 * QUAD, cap, 8 * half), BF)],
        jnp.concatenate([zb, me]),
        got,
        scalars=1,
    )
    slots = got.reshape(rows_all, 8 * half)

    (other,) = kernel_call(
        sibling_kernel,
        [jax.ShapeDtypeStruct((QUAD, cap, 3 * width), BF)],
        core,
        slots,
        *weights,
        scalars=1,
    )
    other = lax.ppermute(other, "core", [(0, 1), (1, 0)])
    total = jax.ShapeDtypeStruct((cap, 3 * width), F32)
    wire = jax.ShapeDtypeStruct((cap, 3 * width), BF)
    far, behind, own, ahead = kernel_call(
        split_kernel,
        [wire] * 2 + [total] * 2,
        jnp.concatenate([core, me]),
        slots,
        *weights,
        other,
        scalars=1,
        scratch=[pltpu.VMEM((QUAD, cap, 3 * width), F32)],
    )
    from_right = shift(behind, -1)
    (to_right,) = kernel_call(relay_kernel, [wire], ahead, shift(far, 1))
    (rows,) = kernel_call(activate_kernel, [wire], own, shift(to_right, 1), from_right)

    rows = lax.all_gather(rows, "za", axis=0, tiled=True)
    rows = lax.all_gather(rows, "core", axis=0, tiled=True)
    (outs,) = kernel_call(
        outs_kernel, [jax.ShapeDtypeStruct((rows_all, 8 * half), BF)], rows, *weights
    )
    outs = outs.reshape(2 * QUAD, cap, 8 * half)
    w_sent = kernel_call(
        grads_kernel,
        [jax.ShapeDtypeStruct((half, 3 * width), F32)]
        + [jax.ShapeDtypeStruct((half, 3 * width), BF)] * 3,
        slots,
        rows,
    )
    (home,) = kernel_call(
        collect_kernel,
        [jax.ShapeDtypeStruct((experts, 2, cap, 2 * half), BF)],
        jnp.concatenate([zb, me]),
        outs,
        w_sent[3],
        scalars=1,
        free=1,
    )
    last_sent, home = lax.optimization_barrier((w_sent[3], home))
    w_grads = (
        w_sent[0],
        along_ring(w_sent[1], (1, 1)),
        along_ring(w_sent[2], (-1, -1)),
        along_ring(last_sent, (2, -2)),
    )

    home = lax.all_to_all(home, PLANE, split_axis=0, concat_axis=0, tiled=True)
    ready = kernel_call(
        combine_kernel,
        [jax.ShapeDtypeStruct((group_rows, 2 * half), BF)] * 2,
        core,
        same,
        cross,
        home,
        scalars=1,
    )
    by_row = jax.ShapeDtypeStruct((1, half, width), F32)
    by_column = jax.ShapeDtypeStruct((1, width, half), F32)
    ends = kernel_call(
        finish_kernel,
        [by_row] * 4 + [by_column] * 2 + [jax.ShapeDtypeStruct((8, 128), F32)],
        *w_grads,
        noise_gate,
        noise_up,
        noise_down,
    )
    mixed_out, token_grad = kernel_call(
        unpack_kernel,
        [jax.ShapeDtypeStruct((group_rows, feats), BF)] * 2,
        core,
        to_window(ready[0], False, True),
        to_window(ready[1], True, True),
        ends[6],
        scalars=1,
        free=1,
    )
    return (mixed_out, token_grad) + tuple(ends[:6])


def solution(mesh):
    fine = Mesh(mesh.devices.reshape(4, 4, QUAD, 4, 2), PLANE + RING)
    by_token = P(RING, PLANE)
    by_group = P(RING, None)
    by_row = P(PLANE, RING, None)
    by_column = P(PLANE, None, RING)
    return jax.shard_map(
        body,
        mesh=fine,
        in_specs=(by_token,) * 2 + (by_group,) * 2 + (by_row,) * 6 + (by_column,) * 3,
        out_specs=(by_token,) * 2 + (by_row,) * 4 + (by_column,) * 2,
        check_vma=False,
    )
```
